32 devices in a mesh: dp: 8 (over z, y), mp: 4 (over x, core).
Axes of the slice: x: 2, y: 2, z: 4, core: 2. Of those that a mesh axis runs over, the one named last changes fastest.
Arguments:
- student: bfloat16 [384, 16, 1280], P('dp'), may hold values from -6 to 6
- dino_target: bfloat16 [256, 16, 1536], P('dp', None, 'mp'), may hold values from -6 to 6
- siglip_target: bfloat16 [256, 16, 1152], P('dp', None, 'mp'), may hold values from -6 to 6
- clip_target: bfloat16 [256, 16, 1024], P('dp', None, 'mp'), may hold values from -6 to 6
- image_owner: int32 [256, 1], replicated, may hold values from 0 to 7; in each aligned block of 32 rows (0 to 31, 32 to 63, ...) at most 6 rows name the same one
- patch_count: int32 [256], replicated, may hold values from 1 to 16
- dino_expand: bfloat16 [1280, 1536], P(None, 'mp'), may hold values from -0.15625 to 0.15625
- dino_project: bfloat16 [1536, 1536], P('mp'), may hold values from -0.15625 to 0.15625
- siglip_expand: bfloat16 [1280, 1536], P(None, 'mp'), may hold values from -0.15625 to 0.15625
- siglip_project: bfloat16 [1536, 1152], P('mp'), may hold values from -0.15625 to 0.15625
- clip_expand: bfloat16 [1280, 1536], P(None, 'mp'), may hold values from -0.15625 to 0.15625
- clip_project: bfloat16 [1536, 1024], P('mp'), may hold values from -0.15625 to 0.15625
Outputs:
- student_grad: bfloat16 [384, 16, 1280], P('dp', None, 'mp')
- dino_expand_grad: float32 [1280, 1536], P('dp', 'mp')
- dino_project_grad: float32 [1536, 1536], P('mp', 'dp')
- siglip_expand_grad: float32 [1280, 1536], P('dp', 'mp')
- siglip_project_grad: float32 [1536, 1152], P('mp', 'dp')
- clip_expand_grad: float32 [1280, 1536], P('dp', 'mp')
- clip_project_grad: float32 [1536, 1024], P('mp', 'dp')
The draws below stay inside these ranges and needn't reach their ends.
Inputs may be any that keep to these rules, and one draw needn't show every extreme that they name: `image_owner`: within each aligned block of 32 images (one store shard) no owner is named more than 6 times; every owner is named by some image.
All inputs are finite; a program needn't handle non-finite values.
Results may differ from the reference program's by a relative error of at most 0.028.
Values may be sent and summed in bfloat16 or wider, within the bound.
A program may use at most 128 MiB of HBM per device.

```python
import math
import jax
import jax.numpy as jnp
import numpy as np
from jax import lax

DS = 1280
ADAPT_H = 1536
DINO_W = 1536
SIGLIP_W = 1152
CLIP_W = 1024
IMG_DEV = 32
PATCHES = 16
CAP = 6
IMAGES = 256
SLOTS = 48
N_DP = 8
N_MP = 4


def with_ends(values, stream_key, least, largest):
    longest = values.shape.index(max(values.shape))
    spots = []
    for shift in (0, 1):
        where = [jax.random.randint(jax.random.fold_in(stream_key, axis), (), 0, length) for axis, length in enumerate(values.shape)]
        where[longest] = (where[longest] + shift) % values.shape[longest]
        spots.append(tuple(where))
    return values.at[spots[0]].set(least).at[spots[1]].set(largest)


def block_levels(key, shape, split, least, largest):
    factor_of = 1.0
    for dim, shards_of in split:
        steps = jax.random.uniform(jax.random.fold_in(jax.random.fold_in(key, 6), dim), (shards_of,), jnp.float32, least / len(split), largest / len(split))
        factor_of = factor_of * jnp.repeat(jnp.exp(steps), shape[dim] // shards_of).reshape((-1,) + (1,) * (len(shape) - 1 - dim))
    return factor_of


def deal_out(stream_key, own, number, rows, count, top, most, slope):
    ranking = jax.random.permutation(stream_key, count)
    packed, usual = load_shares(count, rows * top, most, slope, True), load_shares(count, rows * top, most, slope, False)
    places = jnp.arange(count)

    def named(tallies, rotation):
        used = int((tallies > 0).sum())
        fixed = max(1, used // 4)
        passed = fixed + (places - fixed + rotation * (used - fixed)) % max(1, count - fixed)
        return jnp.zeros((count,), jnp.int32).at[ranking[jnp.where(places < fixed, places, passed)]].set(jnp.asarray(tallies, jnp.int32))

    tallies = jnp.where(number % 4 == 0, named(packed, number // 4), named(usual, number - number // 4 - 1))
    mixed = jax.random.permutation(jax.random.fold_in(own, 3), count)
    donor, receiver = mixed[0:count // 2 * 2:2], mixed[1:count // 2 * 2:2]
    room = jnp.minimum(tallies[donor] - 1, most - tallies[receiver]) // 2
    room = jnp.where((donor == ranking[0]) | (receiver == ranking[0]) | (tallies[receiver] == 0), 0, jnp.maximum(room, 0))
    passed = jax.random.randint(jax.random.fold_in(own, 4), (count // 2,), 0, 1 << 20) % (room + 1)
    tallies = tallies.at[donor].add(-passed).at[receiver].add(passed)
    members = jnp.searchsorted(jnp.cumsum(tallies), jnp.arange(rows * top), side="right").astype(jnp.int32)
    table = members.reshape(top, rows).T
    table = table[jax.random.permutation(jax.random.fold_in(own, 1), rows)]
    rotation = jax.random.randint(jax.random.fold_in(own, 2), (rows, 1), 0, top)
    return jnp.take_along_axis(table, (jnp.arange(top)[None, :] + rotation) % top, axis=1)


def load_shares(number_of, total, bound, lean, full):
    weights = [(1 << 20) // math.isqrt(standing ** lean) + 1 for standing in range(1, number_of + 1)]
    largest = bound if full else min(bound, max(-(-total // number_of), total * weights[0] // sum(weights)))
    least = 1 if total - largest >= number_of - 1 else 0
    holding, rest = [largest] + [least] * (number_of - 1), total - largest - least * (number_of - 1)
    while rest > 0:
        free = [i for i in range(1, number_of) if holding[i] < largest] or [i for i in range(1, number_of) if holding[i] < bound]
        whole, remaining = sum([weights[i] for i in free]), rest
        for i in free:
            extra = min(bound - holding[i], max(1, remaining * weights[i] // whole), rest)
            holding[i] = holding[i] + extra
            rest = rest - extra
    return np.array(holding)


def gaussian(stream_key, extent, deviation, reach, cuts=(), held_as=jnp.bfloat16):
    array = jax.random.normal(stream_key, extent, jnp.float32) * deviation
    if len(cuts) > 0:
        array = block_levels(stream_key, extent, cuts, -0.22, 0.18) * array
    return jnp.clip(array, min=-reach, max=reach).astype(held_as)


def setup_inputs(seed: int = 0) -> dict:
    streams_of = jax.random.split(jax.random.key(seed), 13)
    student = gaussian(streams_of[0], (N_DP * SLOTS, PATCHES, DS), 1.0, 6.0, ((0, 8),))
    dino_target = gaussian(streams_of[1], (IMAGES, PATCHES, DINO_W), 1.0, 6.0, ((0, 8), (2, 4)))
    siglip_target = gaussian(streams_of[2], (IMAGES, PATCHES, SIGLIP_W), 1.0, 6.0, ((0, 8), (2, 4)))
    clip_target = gaussian(streams_of[3], (IMAGES, PATCHES, CLIP_W), 1.0, 6.0, ((0, 8), (2, 4)))
    image_owner_keys = jax.random.split(jax.random.fold_in(streams_of[4], 1), IMAGES // IMG_DEV)
    image_owner_turns = jax.random.permutation(jax.random.fold_in(streams_of[4], 3), IMAGES // IMG_DEV)
    image_owner = jax.vmap(lambda own, number: deal_out(jax.random.fold_in(streams_of[4], 2), own, number, IMG_DEV, N_DP, 1, CAP, 2))(image_owner_keys, image_owner_turns).reshape((IMAGES, 1))
    patch_count = with_ends(jax.random.randint(streams_of[5], (IMAGES,), 1, PATCHES + 1), jax.random.fold_in(streams_of[5], 1), 1, PATCHES).astype(jnp.int32)
    dino_expand = gaussian(streams_of[6], (DS, ADAPT_H), DS ** -0.5, 0.15625, ((1, 4),))
    dino_project = gaussian(streams_of[7], (ADAPT_H, DINO_W), ADAPT_H ** -0.5, 0.15625, ((0, 4),))
    siglip_expand = gaussian(streams_of[8], (DS, ADAPT_H), DS ** -0.5, 0.15625, ((1, 4),))
    siglip_project = gaussian(streams_of[9], (ADAPT_H, SIGLIP_W), ADAPT_H ** -0.5, 0.15625, ((0, 4),))
    clip_expand = gaussian(streams_of[10], (DS, ADAPT_H), DS ** -0.5, 0.15625, ((1, 4),))
    clip_project = gaussian(streams_of[11], (ADAPT_H, CLIP_W), ADAPT_H ** -0.5, 0.15625, ((0, 4),))
    return {"student": student, "dino_target": dino_target, "siglip_target": siglip_target, "clip_target": clip_target, "image_owner": image_owner, "patch_count": patch_count, "dino_expand": dino_expand, "dino_project": dino_project, "siglip_expand": siglip_expand, "siglip_project": siglip_project, "clip_expand": clip_expand, "clip_project": clip_project}


def gelu_parts(hidden):
    normal_cdf = 0.5 * (1.0 + jax.scipy.special.erf(hidden * 0.7071067811865476))
    density = jnp.exp(-0.5 * hidden * hidden) * 0.3989422804014327
    return (hidden * normal_cdf, normal_cdf + hidden * density)

def reference(student, dino_target, siglip_target, clip_target, image_owner, patch_count, dino_expand, dino_project, siglip_expand, siglip_project, clip_expand, clip_project):
    owners = image_owner[:, 0]
    store_owner = owners.reshape(N_DP, IMG_DEV)
    matching = store_owner[:, :, None] == store_owner[:, None, :]
    indices = jnp.arange(IMG_DEV, dtype=jnp.int32)
    earlier = indices[None, :] < indices[:, None]
    position = lax.optimization_barrier(jnp.sum((matching & earlier[None]).astype(jnp.int32), axis=2))
    slot = (store_owner * SLOTS + jnp.arange(N_DP, dtype=jnp.int32)[:, None] * CAP + position).reshape(-1)
    row_total = IMAGES * PATCHES
    x_rows = student[slot].reshape(row_total, DS)
    patch_index = jnp.arange(PATCHES, dtype=jnp.int32)
    valid = (patch_index[None, :] < patch_count[:, None]).astype(jnp.float32).reshape(-1)
    loss_scale = 1.0 / jnp.sqrt(jnp.sum(patch_count).astype(jnp.float32))
    group = ADAPT_H // N_MP
    partials = [jnp.zeros((row_total, DS), jnp.float32) for group_index in range(N_MP)]
    grads = []
    teachers = ((dino_target, dino_expand, dino_project), (siglip_target, siglip_expand, siglip_project), (clip_target, clip_expand, clip_project))
    for target, expand, project in teachers:
        hidden = jnp.dot(x_rows, expand, preferred_element_type=jnp.float32)
        activated, gelu_slope = gelu_parts(hidden)
        activated = activated.astype(jnp.bfloat16)
        adapted = jnp.zeros((row_total, target.shape[2]), jnp.float32)
        for group_index in range(N_MP):
            lower = group_index * group
            partial_out = jnp.dot(activated[:, lower:lower + group], project[lower:lower + group], preferred_element_type=jnp.float32).astype(jnp.bfloat16)
            adapted = adapted + lax.optimization_barrier(partial_out).astype(jnp.float32)
        target_flat = target.reshape(row_total, target.shape[2]).astype(jnp.float32)
        residual = ((adapted - target_flat) * valid[:, None]).astype(jnp.bfloat16)
        back_sum = jnp.dot(residual, project.T, preferred_element_type=jnp.float32)
        hidden_grad = (back_sum * gelu_slope).astype(jnp.bfloat16)
        grads.append(jnp.dot(x_rows.T, hidden_grad, preferred_element_type=jnp.float32) * loss_scale)
        grads.append(jnp.dot(activated.T, residual, preferred_element_type=jnp.float32) * loss_scale)
        for group_index in range(N_MP):
            lower = group_index * group
            partials[group_index] = partials[group_index] + jnp.dot(hidden_grad[:, lower:lower + group], expand[:, lower:lower + group].T, preferred_element_type=jnp.float32)
    summed = jnp.zeros((row_total, DS), jnp.float32)
    for group_index in range(N_MP):
        rounded = lax.optimization_barrier(partials[group_index].astype(jnp.bfloat16))
        summed = summed + rounded.astype(jnp.float32)
    placed = jnp.zeros((N_DP * SLOTS, PATCHES, DS), jnp.bfloat16)
    placed = placed.at[slot].set(summed.astype(jnp.bfloat16).reshape(IMAGES, PATCHES, DS))
    return (placed, grads[0], grads[1], grads[2], grads[3], grads[4], grads[5])
```

```python
import functools

import jax
import jax.numpy as jnp
from jax import lax
from jax.experimental import pallas as pl
from jax.experimental.pallas import tpu as pltpu
from jax.sharding import PartitionSpec as P

MESH = pl.DeviceIdType.MESH
F32 = jnp.float32
BF16 = jnp.bfloat16


def for_sending(value):

    def short(part):
        return part.astype(jnp.bfloat16) if part.dtype == jnp.float32 else part

    return jax.tree.map(short, value)


def gelu_parts(hidden):
    normal_cdf = 0.5 * (1.0 + jax.scipy.special.erf(hidden * 0.7071067811865476))
    density = jnp.exp(-0.5 * hidden * hidden) * 0.3989422804014327
    return (hidden * normal_cdf, normal_cdf + hidden * density)


def selection(store_block, owner_ids, capacity):
    belongs = (owner_ids[:, None] == store_block[None, :]).astype(jnp.int32)
    position = jnp.cumsum(belongs, axis=1) - 1
    ranks = jnp.arange(capacity, dtype=jnp.int32)
    return belongs[:, None, :] * (position[:, None, :] == ranks[None, :, None]).astype(jnp.int32)


def fold_step(activated, project, segment):
    back_sum = lax.dot_general(
        segment, project, (((1,), (1,)), ((), ())), preferred_element_type=jnp.float32
    )
    update = lax.dot_general(
        activated, segment, (((0,), (0,)), ((), ())), preferred_element_type=jnp.float32
    )
    return (back_sum, update)


def first_term(inputs, hidden_grad, loss_scale):
    return (
        lax.dot_general(
            inputs, hidden_grad, (((0,), (0,)), ((), ())), preferred_element_type=jnp.float32
        )
        * loss_scale
    )


def adapt(inputs, targets, slot_counts, weights, loss_scale):
    positions = jnp.arange(targets[0].shape[2], dtype=jnp.int32)
    valid_mask = (
        (positions[None, None, :] < slot_counts[:, :, None]).astype(jnp.float32).reshape(-1)
    )
    student_part = jnp.zeros(inputs.shape, jnp.float32)
    results = []
    for target, weight_pair in zip(targets, weights):
        expand, project = weight_pair
        hidden = jnp.dot(inputs, expand, preferred_element_type=jnp.float32)
        activated, gelu_slope = gelu_parts(hidden)
        activated = activated.astype(jnp.bfloat16)
        adapted = lax.psum_scatter(
            jnp.dot(activated, project, preferred_element_type=jnp.float32).astype(jnp.bfloat16),
            "mp",
            scatter_dimension=1,
            tiled=True,
        ).astype(jnp.float32)
        target_flat = target.reshape(-1, target.shape[3]).astype(jnp.float32)
        residual = ((adapted - target_flat) * valid_mask[:, None]).astype(jnp.bfloat16)
        back_sum, project_grad = fold_step(
            activated, project, lax.all_gather(residual, "mp", axis=1, tiled=True)
        )
        hidden_grad = (back_sum * gelu_slope).astype(jnp.bfloat16)
        expand_grad = lax.psum_scatter(
            first_term(inputs, hidden_grad, loss_scale).astype(jnp.bfloat16),
            "dp",
            scatter_dimension=0,
            tiled=True,
        ).astype(jnp.float32)
        project_grad = lax.psum_scatter(
            (project_grad * loss_scale).astype(jnp.bfloat16), "dp", scatter_dimension=1, tiled=True
        ).astype(jnp.float32)
        student_part = student_part + lax.dot_general(
            hidden_grad, expand, (((1,), (1,)), ((), ())), preferred_element_type=jnp.float32
        )
        results.append(expand_grad)
        results.append(project_grad)
    return (student_part, results)


def shards(
    student,
    dino_target,
    siglip_target,
    clip_target,
    image_owner,
    patch_count,
    dino_expand,
    dino_project,
    siglip_expand,
    siglip_project,
    clip_expand,
    clip_project,
):
    stores = lax.axis_size("dp")
    store_index = lax.axis_index("dp")
    per_store = dino_target.shape[0]
    patches = dino_target.shape[1]
    slot_total = student.shape[0]
    capacity = slot_total // stores
    owners = image_owner[:, 0]
    store_owner = owners.reshape(stores, per_store)
    counts_store = patch_count.reshape(stores, per_store)
    loss_scale = 1.0 / jnp.sqrt(jnp.sum(patch_count).astype(jnp.float32))
    own_block = lax.dynamic_slice_in_dim(owners, store_index * per_store, per_store)
    sel_store = selection(own_block, jnp.arange(stores, dtype=jnp.int32), capacity)
    picker = sel_store.astype(jnp.bfloat16)
    teachers = (dino_target, siglip_target, clip_target)
    weights = (
        (dino_expand, dino_project),
        (siglip_expand, siglip_project),
        (clip_expand, clip_project),
    )
    outgoing = tuple(
        (
            jnp.einsum("oki,ipf->okpf", picker, teacher, preferred_element_type=jnp.float32).astype(
                jnp.bfloat16
            )
            for teacher in teachers
        )
    )
    targets = jax.tree.map(
        lambda part, own: part.astype(own.dtype),
        lax.all_to_all(for_sending(outgoing), "dp", split_axis=0, concat_axis=0, tiled=True),
        outgoing,
    )
    owner_key = jnp.reshape(store_index, (1,))
    sel_owner = jax.vmap(lambda store_block: selection(store_block, owner_key, capacity)[0])(
        store_owner
    )
    slot_counts = jnp.sum(sel_owner * counts_store[:, None, :], axis=2)
    inputs = student.reshape(-1, student.shape[2])
    student_part, results = adapt(inputs, targets, slot_counts, weights, loss_scale)
    student_grad = lax.psum_scatter(
        student_part.reshape(slot_total, patches, -1).astype(jnp.bfloat16),
        "mp",
        scatter_dimension=2,
        tiled=True,
    )
    return (student_grad, results[0], results[1], results[2], results[3], results[4], results[5])


def nn(a, b):
    return lax.dot_general(a, b, (((1,), (0,)), ((), ())), preferred_element_type=F32)


def nt(a, b):
    return lax.dot_general(a, b, (((1,), (1,)), ((), ())), preferred_element_type=F32)


def tn(a, b):
    return lax.dot_general(a, b, (((0,), (0,)), ((), ())), preferred_element_type=F32)


def rows_at(index, size):
    return pl.ds(pl.multiple_of(index * size, 16), size)


def fused_kernel(names, orders, *refs):
    r = dict(zip(names, refs))
    dp, mp = lax.axis_index("dp"), lax.axis_index("mp")
    x, core = mp // 2, mp % 2
    sibling = mp + 1 - 2 * core
    across = mp + 2 - 4 * x
    n_dp, n_mp = 8, 4
    sent = []
    numbers = iter(range(r["ssem"].shape[0]))

    def send(source, landing, device):
        number = next(numbers)
        copy = pltpu.make_async_remote_copy(
            src_ref=source,
            dst_ref=landing,
            send_sem=r["ssem"].at[number],
            recv_sem=r["rsem"].at[number],
            device_id=device,
            device_id_type=MESH,
        )
        copy.start()
        sent.append(copy)
        return copy

    dp_peers = [lax.rem(dp + k, n_dp) for k in range(1, n_dp)]
    barrier = pltpu.get_barrier_semaphore()
    for peer in dp_peers:
        pl.semaphore_signal(barrier, inc=1, device_id=(peer, mp), device_id_type=MESH)
    for peer in (sibling, across):
        pl.semaphore_signal(barrier, inc=1, device_id=(dp, peer), device_id_type=MESH)
    pl.semaphore_wait(barrier, n_dp + 1)

    xs, xr, xt = r["xs"], r["xr"], r["xt"]
    quarter = xt.shape[0] // n_mp
    slot_rows, row_total = xr.shape[0] * xr.shape[1], xt.shape[1]
    arrivals = [send(xs.at[peer], xr.at[dp], (peer, mp)) for peer in dp_peers]
    xr[dp] = xs[dp]
    picked = lax.broadcasted_iota(jnp.int32, (slot_rows, row_total), 0) == r["place"][...]
    r["sel"][...] = picked.astype(F32).astype(BF16)
    for copy in arrivals:
        copy.wait_recv()
    mine = rows_at(mp, quarter)
    theirs = rows_at(across, quarter)
    xt[mine, :] = tn(xr[...].reshape(slot_rows, quarter), r["sel"][...]).astype(BF16)
    to_sibling = send(xt.at[mine, :], xt.at[mine, :], (dp, sibling))
    to_across = send(xt.at[mine, :], xt.at[mine, :], (dp, across))
    to_across.wait_recv()
    forward = send(xt.at[theirs, :], xt.at[theirs, :], (dp, sibling))
    to_sibling.wait_recv()
    forward.wait_recv()

    teachers = range(3)
    core_copy, x_copy, gather = {}, {}, {}

    def first_half(t):
        expand, project_t = r[f"expand{t}"], r[f"project_t{t}"]
        hidden = tn(expand[...], xt[...])
        cdf = 0.5 * (1.0 + lax.erf(hidden * 0.7071067811865476))
        density = jnp.exp(-0.5 * hidden * hidden) * 0.3989422804014327
        r[f"slope{t}"][...] = cdf + hidden * density
        r[f"act{t}"][...] = (hidden * cdf).astype(BF16)
        part = r[f"part{t}"]
        width = part.shape[2]

        def block(j, carry):
            part[j % 2, j // 2] = nn(
                project_t[rows_at(j, width), :], r[f"act{t}"][...]
            ).astype(BF16)
            return carry

        lax.fori_loop(0, n_mp, block, 0)
        core_copy[t] = send(part.at[1 - core], r[f"from_core{t}"], (dp, sibling))

    def to_x(t):
        part, landed = r[f"part{t}"], r[f"from_core{t}"]
        core_copy[t].wait_recv()
        part[core, 1 - x] = (
            part[core, 1 - x].astype(F32) + landed[1 - x].astype(F32)
        ).astype(BF16)
        x_copy[t] = send(part.at[core, 1 - x], r[f"from_x{t}"], (dp, across))

    def residual(t):
        part, landed, res = r[f"part{t}"], r[f"from_core{t}"], r[f"res{t}"]
        width = part.shape[2]
        own = part[core, x].astype(F32) + landed[x].astype(F32)
        x_copy[t].wait_recv()
        adapted = own + r[f"from_x{t}"][...].astype(F32)
        here = rows_at(mp, width)
        res[here, :] = ((adapted - r[f"target{t}"][...].astype(F32)) * r["valid"][...]).astype(BF16)
        near = send(res.at[here, :], res.at[here, :], (dp, sibling))
        far = send(res.at[here, :], res.at[here, :], (dp, across))
        gather[t] = (near, far)

    def pass_on(t):
        res = r[f"res{t}"]
        there = rows_at(across, r[f"part{t}"].shape[2])
        near, far = gather[t]
        far.wait_recv()
        gather[t] = (near, send(res.at[there, :], res.at[there, :], (dp, sibling)))

    def bit_of(index, bit):
        return (index // bit) % 2

    def partner(bit):
        return dp + bit - 2 * bit * bit_of(dp, bit)

    stage = {}

    def start_reduce(i):
        total, order = r[f"sum{i}"], orders[i]
        stage[i] = send(
            total.at[1 - bit_of(dp, order[0])], r[f"first{i}"], (partner(order[0]), mp)
        )

    def second(i):
        total, landed, order = r[f"sum{i}"], r[f"first{i}"], orders[i]
        own = bit_of(dp, order[0])
        stage[i].wait_recv()

        def block(k, carry):
            a, b = k // 2, k % 2
            total[own, a, b] = (
                total[own, a, b].astype(F32) + landed[a, b].astype(F32)
            ).astype(BF16)
            return carry

        lax.fori_loop(0, 4, block, 0)
        stage[i] = send(
            total.at[own, 1 - bit_of(dp, order[1])], r[f"next{i}"], (partner(order[1]), mp)
        )

    def third(i):
        total, landed, order = r[f"sum{i}"], r[f"next{i}"], orders[i]
        own, mid = bit_of(dp, order[0]), bit_of(dp, order[1])
        stage[i].wait_recv()

        def block(k, carry):
            total[own, mid, k] = (
                total[own, mid, k].astype(F32) + landed[k].astype(F32)
            ).astype(BF16)
            return carry

        lax.fori_loop(0, 2, block, 0)
        stage[i] = send(
            total.at[own, mid, 1 - bit_of(dp, order[2])], r[f"last{i}"], (partner(order[2]), mp)
        )

    def finish(i):
        total, order = r[f"sum{i}"], orders[i]
        own = [bit_of(dp, bit) for bit in order]
        stage[i].wait_recv()
        r[f"out{i}"][...] = (
            total[own[0], own[1], own[2]].astype(F32) + r[f"last{i}"][...].astype(F32)
        ) * r["scale"][...]

    def grads(t):
        res, act, grad = r[f"res{t}"], r[f"act{t}"], r[f"grad{t}"]
        near, forwarded = gather[t]
        near.wait_recv()
        forwarded.wait_recv()
        for i, left, right in ((2 * t, res, act), (2 * t + 1, xt, grad)):
            total, order = r[f"sum{i}"], orders[i]
            size = total.shape[3]
            if right is grad:
                back = nn(r[f"project{t}"][...], res[...])
                grad[...] = (back * r[f"slope{t}"][...]).astype(BF16)

            def block(k, carry):
                place = [bit_of(k, bit) for bit in order]
                total[place[0], place[1], place[2]] = nt(
                    left[rows_at(k, size), :], right[...]
                ).astype(BF16)
                return carry

            lax.fori_loop(0, n_dp, block, 0)
            start_reduce(i)

    first_half(0)
    first_half(1)
    to_x(0)
    first_half(2)
    to_x(1)
    residual(0)
    to_x(2)
    residual(1)
    pass_on(0)
    grads(0)
    residual(2)
    pass_on(1)
    pass_on(2)
    grads(1)
    second(0)
    second(1)
    grads(2)

    sp = r["sp"]

    def block(j, carry):
        sp[j % 2, j // 2] = sum(
            nn(r[f"expand{t}"][rows_at(j, quarter), :], r[f"grad{t}"][...]) for t in teachers
        ).astype(BF16)
        return carry

    lax.fori_loop(0, n_mp, block, 0)
    core_copy["s"] = send(sp.at[1 - core], r["sp_core"], (dp, sibling))
    third(0)
    second(2)
    third(1)
    core_copy["s"].wait_recv()
    sp[core, 1 - x] = (
        sp[core, 1 - x].astype(F32) + r["sp_core"][1 - x].astype(F32)
    ).astype(BF16)
    x_copy["s"] = send(sp.at[core, 1 - x], r["sp_x"], (dp, across))
    second(3)
    third(2)
    finish(0)
    own = sp[core, x].astype(F32) + r["sp_core"][x].astype(F32)
    x_copy["s"].wait_recv()
    summed = (own + r["sp_x"][...].astype(F32)).astype(BF16)
    placed = nt(r["sel"][...], summed).astype(BF16)
    r["home"][...] = placed.reshape(r["home"].shape)
    returns = [
        send(r["home"].at[peer], r["student_out"].at[dp], (peer, mp)) for peer in dp_peers
    ]
    r["student_out"][dp] = r["home"][dp]
    second(4)
    third(3)
    finish(1)
    second(5)
    third(4)
    finish(2)
    third(5)
    finish(3)
    finish(4)
    finish(5)
    for copy in returns:
        copy.wait_recv()
    for copy in sent:
        copy.wait_send()


def fused(
    student,
    dino_target,
    siglip_target,
    clip_target,
    image_owner,
    patch_count,
    dino_expand,
    dino_project,
    siglip_expand,
    siglip_project,
    clip_expand,
    clip_project,
):
    stores, groups = lax.axis_size("dp"), lax.axis_size("mp")
    dp, mp = lax.axis_index("dp"), lax.axis_index("mp")
    per_store, patches = dino_target.shape[0], dino_target.shape[1]
    capacity = student.shape[0] // stores
    width = student.shape[2]
    quarter = width // groups
    rows = per_store * patches
    owners = lax.dynamic_slice_in_dim(image_owner[:, 0], dp * per_store, per_store)
    counts = lax.dynamic_slice_in_dim(patch_count, dp * per_store, per_store)
    index = jnp.arange(per_store, dtype=jnp.int32)
    earlier = (index[None, :] < index[:, None]) & (owners[None, :] == owners[:, None])
    slot = owners * capacity + jnp.sum(earlier.astype(jnp.int32), axis=1)
    patch = jnp.arange(patches, dtype=jnp.int32)
    place = (slot[:, None] * patches + patch[None, :]).reshape(1, rows)
    valid = (patch[None, :] < counts[:, None]).astype(F32).reshape(1, rows)
    loss_scale = 1.0 / jnp.sqrt(jnp.sum(patch_count).astype(F32))
    hidden = dino_expand.shape[1]
    scale = jnp.broadcast_to(loss_scale, (1, hidden))
    xs = lax.dynamic_slice_in_dim(
        student.reshape(stores, capacity * patches, width), mp * quarter, quarter, axis=2
    )
    expands = (dino_expand, siglip_expand, clip_expand)
    projects = (dino_project, siglip_project, clip_project)
    targets = (dino_target, siglip_target, clip_target)

    inputs = {"xs": xs, "place": place, "valid": valid, "scale": scale}
    outputs = {"student_out": jax.ShapeDtypeStruct(xs.shape, BF16)}
    scratch = {
        "ssem": pltpu.SemaphoreType.DMA((52,)),
        "rsem": pltpu.SemaphoreType.DMA((52,)),
        "xr": pltpu.VMEM(xs.shape, BF16),
        "home": pltpu.VMEM(xs.shape, BF16),
        "xt": pltpu.VMEM((width, rows), BF16),
        "sel": pltpu.VMEM((stores * capacity * patches, rows), BF16),
        "sp": pltpu.VMEM((2, 2, quarter, rows), BF16),
        "sp_core": pltpu.VMEM((2, quarter, rows), BF16),
        "sp_x": pltpu.VMEM((quarter, rows), BF16),
    }
    orders = []
    for t, (target, expand, project) in enumerate(zip(targets, expands, projects)):
        columns = target.shape[2]
        features = project.shape[1]
        inputs[f"target{t}"] = target.reshape(rows, columns).T
        inputs[f"expand{t}"] = expand
        inputs[f"project{t}"] = project
        inputs[f"project_t{t}"] = project.T
        scratch[f"slope{t}"] = pltpu.VMEM((hidden, rows), F32)
        scratch[f"act{t}"] = pltpu.VMEM((hidden, rows), BF16)
        scratch[f"grad{t}"] = pltpu.VMEM((hidden, rows), BF16)
        scratch[f"part{t}"] = pltpu.VMEM((2, 2, columns, rows), BF16)
        scratch[f"from_core{t}"] = pltpu.VMEM((2, columns, rows), BF16)
        scratch[f"from_x{t}"] = pltpu.VMEM((columns, rows), BF16)
        scratch[f"res{t}"] = pltpu.VMEM((features, rows), BF16)
        for i, size in ((2 * t, features // stores), (2 * t + 1, width // stores)):
            outputs[f"out{i}"] = jax.ShapeDtypeStruct((size, hidden), F32)
            scratch[f"sum{i}"] = pltpu.VMEM((2, 2, 2, size, hidden), BF16)
            scratch[f"first{i}"] = pltpu.VMEM((2, 2, size, hidden), BF16)
            scratch[f"next{i}"] = pltpu.VMEM((2, size, hidden), BF16)
            scratch[f"last{i}"] = pltpu.VMEM((size, hidden), BF16)
            orders.append((2, 1, 4) if i == 2 else (1, 2, 4))
    names = list(inputs) + list(outputs) + list(scratch)
    vmem = pl.BlockSpec(memory_space=pltpu.VMEM)
    features = sum(project.shape[1] for project in projects)
    results = pl.pallas_call(
        functools.partial(fused_kernel, names, orders),
        out_shape=tuple(outputs.values()),
        in_specs=[vmem] * len(inputs),
        out_specs=tuple([vmem] * len(outputs)),
        scratch_shapes=list(scratch.values()),
        compiler_params=pltpu.CompilerParams(
            collective_id=0, has_side_effects=True, vmem_limit_bytes=60 * 1024 * 1024
        ),
        cost_estimate=pl.CostEstimate(
            flops=6 * rows * hidden * (features + 3 * width),
            bytes_accessed=16 * 1024 * 1024,
            transcendentals=6 * rows * hidden,
        ),
    )(*inputs.values())
    student_grad = results[0].reshape(student.shape[0], patches, quarter)
    return (
        student_grad,
        results[2],
        results[1].T,
        results[4],
        results[3].T,
        results[6],
        results[5].T,
    )


def kernel_fits(mesh):
    return mesh.shape["dp"] == 8 and mesh.shape["mp"] == 4


def solution(mesh):
    return jax.shard_map(
        fused if kernel_fits(mesh) else shards,
        mesh=mesh,
        in_specs=(
            P("dp", None, None),
            P("dp", None, "mp"),
            P("dp", None, "mp"),
            P("dp", None, "mp"),
            P(),
            P(),
            P(None, "mp"),
            P("mp", None),
            P(None, "mp"),
            P("mp", None),
            P(None, "mp"),
            P("mp", None),
        ),
        out_specs=(
            P("dp", None, "mp"),
            P("dp", "mp"),
            P("mp", "dp"),
            P("dp", "mp"),
            P("mp", "dp"),
            P("dp", "mp"),
            P("mp", "dp"),
        ),
        check_vma=False,
    )
```

```python
import functools

import jax
import jax.numpy as jnp
from jax import lax
from jax.experimental import pallas as pl
from jax.experimental.pallas import tpu as pltpu
from jax.sharding import PartitionSpec as P

MESH = pl.DeviceIdType.MESH
F32 = jnp.float32
BF16 = jnp.bfloat16


def for_sending(value):

    def short(part):
        return part.astype(jnp.bfloat16) if part.dtype == jnp.float32 else part

    return jax.tree.map(short, value)


def gelu_parts(hidden):
    normal_cdf = 0.5 * (1.0 + jax.scipy.special.erf(hidden * 0.7071067811865476))
    density = jnp.exp(-0.5 * hidden * hidden) * 0.3989422804014327
    return (hidden * normal_cdf, normal_cdf + hidden * density)


def selection(store_block, owner_ids, capacity):
    belongs = (owner_ids[:, None] == store_block[None, :]).astype(jnp.int32)
    position = jnp.cumsum(belongs, axis=1) - 1
    ranks = jnp.arange(capacity, dtype=jnp.int32)
    return belongs[:, None, :] * (position[:, None, :] == ranks[None, :, None]).astype(jnp.int32)


def fold_step(activated, project, segment):
    back_sum = lax.dot_general(
        segment, project, (((1,), (1,)), ((), ())), preferred_element_type=jnp.float32
    )
    update = lax.dot_general(
        activated, segment, (((0,), (0,)), ((), ())), preferred_element_type=jnp.float32
    )
    return (back_sum, update)


def first_term(inputs, hidden_grad, loss_scale):
    return (
        lax.dot_general(
            inputs, hidden_grad, (((0,), (0,)), ((), ())), preferred_element_type=jnp.float32
        )
        * loss_scale
    )


def adapt(inputs, targets, slot_counts, weights, loss_scale):
    positions = jnp.arange(targets[0].shape[2], dtype=jnp.int32)
    valid_mask = (
        (positions[None, None, :] < slot_counts[:, :, None]).astype(jnp.float32).reshape(-1)
    )
    student_part = jnp.zeros(inputs.shape, jnp.float32)
    results = []
    for target, weight_pair in zip(targets, weights):
        expand, project = weight_pair
        hidden = jnp.dot(inputs, expand, preferred_element_type=jnp.float32)
        activated, gelu_slope = gelu_parts(hidden)
        activated = activated.astype(jnp.bfloat16)
        adapted = lax.psum_scatter(
            jnp.dot(activated, project, preferred_element_type=jnp.float32).astype(jnp.bfloat16),
            "mp",
            scatter_dimension=1,
            tiled=True,
        ).astype(jnp.float32)
        target_flat = target.reshape(-1, target.shape[3]).astype(jnp.float32)
        residual = ((adapted - target_flat) * valid_mask[:, None]).astype(jnp.bfloat16)
        back_sum, project_grad = fold_step(
            activated, project, lax.all_gather(residual, "mp", axis=1, tiled=True)
        )
        hidden_grad = (back_sum * gelu_slope).astype(jnp.bfloat16)
        expand_grad = lax.psum_scatter(
            first_term(inputs, hidden_grad, loss_scale).astype(jnp.bfloat16),
            "dp",
            scatter_dimension=0,
            tiled=True,
        ).astype(jnp.float32)
        project_grad = lax.psum_scatter(
            (project_grad * loss_scale).astype(jnp.bfloat16), "dp", scatter_dimension=1, tiled=True
        ).astype(jnp.float32)
        student_part = student_part + lax.dot_general(
            hidden_grad, expand, (((1,), (1,)), ((), ())), preferred_element_type=jnp.float32
        )
        results.append(expand_grad)
        results.append(project_grad)
    return (student_part, results)


def shards(
    student,
    dino_target,
    siglip_target,
    clip_target,
    image_owner,
    patch_count,
    dino_expand,
    dino_project,
    siglip_expand,
    siglip_project,
    clip_expand,
    clip_project,
):
    stores = lax.axis_size("dp")
    store_index = lax.axis_index("dp")
    per_store = dino_target.shape[0]
    patches = dino_target.shape[1]
    slot_total = student.shape[0]
    capacity = slot_total // stores
    owners = image_owner[:, 0]
    store_owner = owners.reshape(stores, per_store)
    counts_store = patch_count.reshape(stores, per_store)
    loss_scale = 1.0 / jnp.sqrt(jnp.sum(patch_count).astype(jnp.float32))
    own_block = lax.dynamic_slice_in_dim(owners, store_index * per_store, per_store)
    sel_store = selection(own_block, jnp.arange(stores, dtype=jnp.int32), capacity)
    picker = sel_store.astype(jnp.bfloat16)
    teachers = (dino_target, siglip_target, clip_target)
    weights = (
        (dino_expand, dino_project),
        (siglip_expand, siglip_project),
        (clip_expand, clip_project),
    )
    outgoing = tuple(
        (
            jnp.einsum("oki,ipf->okpf", picker, teacher, preferred_element_type=jnp.float32).astype(
                jnp.bfloat16
            )
            for teacher in teachers
        )
    )
    targets = jax.tree.map(
        lambda part, own: part.astype(own.dtype),
        lax.all_to_all(for_sending(outgoing), "dp", split_axis=0, concat_axis=0, tiled=True),
        outgoing,
    )
    owner_key = jnp.reshape(store_index, (1,))
    sel_owner = jax.vmap(lambda store_block: selection(store_block, owner_key, capacity)[0])(
        store_owner
    )
    slot_counts = jnp.sum(sel_owner * counts_store[:, None, :], axis=2)
    inputs = student.reshape(-1, student.shape[2])
    student_part, results = adapt(inputs, targets, slot_counts, weights, loss_scale)
    student_grad = lax.psum_scatter(
        student_part.reshape(slot_total, patches, -1).astype(jnp.bfloat16),
        "mp",
        scatter_dimension=2,
        tiled=True,
    )
    return (student_grad, results[0], results[1], results[2], results[3], results[4], results[5])


def nn(a, b):
    return lax.dot_general(a, b, (((1,), (0,)), ((), ())), preferred_element_type=F32)


def nt(a, b):
    return lax.dot_general(a, b, (((1,), (1,)), ((), ())), preferred_element_type=F32)


def tn(a, b):
    return lax.dot_general(a, b, (((0,), (0,)), ((), ())), preferred_element_type=F32)


def rows_at(index, size):
    return pl.ds(pl.multiple_of(index * size, 16), size)


def fused_kernel(names, names_loaded, orders, capacity, patches, *refs):
    r = dict(zip(names, refs))
    dp, mp = lax.axis_index("dp"), lax.axis_index("mp")
    x, core = mp // 2, mp % 2
    sibling = mp + 1 - 2 * core
    across = mp + 2 - 4 * x
    n_dp, n_mp = 8, 4
    sent = []
    numbers = iter(range(r["ssem"].shape[0]))

    def send(source, landing, device):
        number = next(numbers)
        copy = pltpu.make_async_remote_copy(
            src_ref=source,
            dst_ref=landing,
            send_sem=r["ssem"].at[number],
            recv_sem=r["rsem"].at[number],
            device_id=device,
            device_id_type=MESH,
        )
        copy.start()
        sent.append(copy)
        return copy

    loads = {}
    for number, name in enumerate(names_loaded):
        loads[name] = pltpu.make_async_copy(r[name + "_hbm"], r[name], r["lsem"].at[number])
        loads[name].start()

    dp_peers = [lax.rem(dp + k, n_dp) for k in range(1, n_dp)]
    barrier = pltpu.get_barrier_semaphore()
    for peer in dp_peers:
        pl.semaphore_signal(barrier, inc=1, device_id=(peer, mp), device_id_type=MESH)
    for peer in (sibling, across):
        pl.semaphore_signal(barrier, inc=1, device_id=(dp, peer), device_id_type=MESH)
    pl.semaphore_wait(barrier, n_dp + 1)

    xs, xr, xt = r["xs"], r["xr"], r["xt"]
    quarter = xt.shape[0] // n_mp
    slot_rows, row_total = xr.shape[0] * xr.shape[1], xt.shape[1]
    arrivals = [send(xs.at[peer], xr.at[dp], (peer, mp)) for peer in dp_peers]
    xr[dp] = xs[dp]

    owners, counts = r["owners"][...], r["counts"][...]
    images = owners.shape[1]
    per_store = row_total // patches
    first_image = dp * per_store
    image = lax.broadcasted_iota(jnp.int32, (images, row_total), 0) - first_image
    column = lax.broadcasted_iota(jnp.int32, (images, row_total), 1)
    at_column = column // patches
    same = (image == at_column).astype(F32).astype(BF16)
    before = ((image >= 0) & (image < at_column)).astype(F32).astype(BF16)
    padded = jnp.broadcast_to(owners, (8, images))
    owner_of = nn(padded.astype(F32).astype(BF16), same)
    count_of = nn(jnp.broadcast_to(counts, (8, images)).astype(F32).astype(BF16), same)
    named = lax.broadcasted_iota(jnp.int32, (n_dp, images), 0) == padded
    ranks = nn(named.astype(F32).astype(BF16), before)
    ours = lax.broadcasted_iota(jnp.int32, (n_dp, row_total), 0) == owner_of.astype(jnp.int32)
    rank = jnp.sum(jnp.where(ours, ranks, 0.0), axis=0, keepdims=True)
    patch = column[:1] - at_column[:1] * patches
    slot = owner_of[:1].astype(jnp.int32) * capacity + rank.astype(jnp.int32)
    r["valid"][...] = (patch < count_of[:1].astype(jnp.int32)).astype(F32)
    total = jnp.sum(counts.astype(F32), axis=1, keepdims=True)
    r["scale"][...] = jnp.broadcast_to(1.0 / jnp.sqrt(total), r["scale"].shape)
    place = slot * patches + patch
    picked = lax.broadcasted_iota(jnp.int32, (slot_rows, row_total), 0) == place
    r["sel"][...] = picked.astype(F32).astype(BF16)
    for name in names_loaded:
        loads[name].wait()
    for t in range(3):
        r[f"expand_t{t}"][...] = r[f"expand{t}"][...].T
        r[f"project_t{t}"][...] = r[f"project{t}"][...].T
        r[f"target_t{t}"][...] = r[f"target{t}"][...].T
    for copy in arrivals:
        copy.wait_recv()
    mine = rows_at(mp, quarter)
    theirs = rows_at(across, quarter)
    xt[mine, :] = tn(xr[...].reshape(slot_rows, quarter), r["sel"][...]).astype(BF16)
    to_sibling = send(xt.at[mine, :], xt.at[mine, :], (dp, sibling))
    to_across = send(xt.at[mine, :], xt.at[mine, :], (dp, across))
    to_across.wait_recv()
    forward = send(xt.at[theirs, :], xt.at[theirs, :], (dp, sibling))
    to_sibling.wait_recv()
    forward.wait_recv()

    teachers = range(3)
    core_copy, x_copy, gather = {}, {}, {}

    def first_half(t):
        project_t = r[f"project_t{t}"]
        hidden = nn(r[f"expand_t{t}"][...], xt[...])
        cdf = 0.5 * (1.0 + lax.erf(hidden * 0.7071067811865476))
        density = jnp.exp(-0.5 * hidden * hidden) * 0.3989422804014327
        r[f"slope{t}"][...] = cdf + hidden * density
        r[f"act{t}"][...] = (hidden * cdf).astype(BF16)
        part = r[f"part{t}"]
        width = part.shape[2]

        def block(j, carry):
            part[j % 2, j // 2] = nn(
                project_t[rows_at(j, width), :], r[f"act{t}"][...]
            ).astype(BF16)
            return carry

        lax.fori_loop(0, n_mp, block, 0)
        core_copy[t] = send(part.at[1 - core], r[f"from_core{t}"], (dp, sibling))

    def to_x(t):
        part, landed = r[f"part{t}"], r[f"from_core{t}"]
        core_copy[t].wait_recv()
        part[core, 1 - x] = (
            part[core, 1 - x].astype(F32) + landed[1 - x].astype(F32)
        ).astype(BF16)
        x_copy[t] = send(part.at[core, 1 - x], r[f"from_x{t}"], (dp, across))

    def residual(t):
        part, landed, res = r[f"part{t}"], r[f"from_core{t}"], r[f"res{t}"]
        width = part.shape[2]
        own = part[core, x].astype(F32) + landed[x].astype(F32)
        x_copy[t].wait_recv()
        adapted = own + r[f"from_x{t}"][...].astype(F32)
        here = rows_at(mp, width)
        res[here, :] = ((adapted - r[f"target_t{t}"][...].astype(F32)) * r["valid"][...]).astype(BF16)
        near = send(res.at[here, :], res.at[here, :], (dp, sibling))
        far = send(res.at[here, :], res.at[here, :], (dp, across))
        gather[t] = (near, far)

    def pass_on(t):
        res = r[f"res{t}"]
        there = rows_at(across, r[f"part{t}"].shape[2])
        near, far = gather[t]
        far.wait_recv()
        gather[t] = (near, send(res.at[there, :], res.at[there, :], (dp, sibling)))

    def bit_of(index, bit):
        return (index // bit) % 2

    def partner(bit):
        return dp + bit - 2 * bit * bit_of(dp, bit)

    stage = {}

    def start_reduce(i):
        total, order = r[f"sum{i}"], orders[i]
        stage[i] = send(
            total.at[1 - bit_of(dp, order[0])], r[f"first{i}"], (partner(order[0]), mp)
        )

    def second(i):
        total, landed, order = r[f"sum{i}"], r[f"first{i}"], orders[i]
        own = bit_of(dp, order[0])
        stage[i].wait_recv()

        def block(k, carry):
            a, b = k // 2, k % 2
            total[own, a, b] = (
                total[own, a, b].astype(F32) + landed[a, b].astype(F32)
            ).astype(BF16)
            return carry

        lax.fori_loop(0, 4, block, 0)
        stage[i] = send(
            total.at[own, 1 - bit_of(dp, order[1])], r[f"next{i}"], (partner(order[1]), mp)
        )

    def third(i):
        total, landed, order = r[f"sum{i}"], r[f"next{i}"], orders[i]
        own, mid = bit_of(dp, order[0]), bit_of(dp, order[1])
        stage[i].wait_recv()

        def block(k, carry):
            total[own, mid, k] = (
                total[own, mid, k].astype(F32) + landed[k].astype(F32)
            ).astype(BF16)
            return carry

        lax.fori_loop(0, 2, block, 0)
        stage[i] = send(
            total.at[own, mid, 1 - bit_of(dp, order[2])], r[f"last{i}"], (partner(order[2]), mp)
        )

    def finish(i):
        total, order = r[f"sum{i}"], orders[i]
        own = [bit_of(dp, bit) for bit in order]
        stage[i].wait_recv()
        summed = (
            total[own[0], own[1], own[2]].astype(F32) + r[f"last{i}"][...].astype(F32)
        ) * r["scale"][...]
        r[f"out{i}"][...] = summed.T if i % 2 == 0 else summed

    def grads(t):
        res, act, grad = r[f"res{t}"], r[f"act{t}"], r[f"grad{t}"]
        near, forwarded = gather[t]
        near.wait_recv()
        forwarded.wait_recv()
        for i, left, right in ((2 * t, res, act), (2 * t + 1, xt, grad)):
            total, order = r[f"sum{i}"], orders[i]
            size = total.shape[3]
            if right is grad:
                back = nn(r[f"project{t}"][...], res[...])
                grad[...] = (back * r[f"slope{t}"][...]).astype(BF16)

            def block(k, carry):
                both = nt(left[rows_at(k, 2 * size), :], right[...]).astype(BF16)
                for low in (0, 1):
                    at = [bit_of(2 * k + low, bit) for bit in order]
                    total[at[0], at[1], at[2]] = both[low * size : (low + 1) * size]
                return carry

            lax.fori_loop(0, n_dp // 2, block, 0)
            start_reduce(i)

    first_half(0)
    to_x(0)
    first_half(1)
    residual(0)
    to_x(1)
    first_half(2)
    pass_on(0)
    residual(1)
    to_x(2)
    grads(0)
    pass_on(1)
    residual(2)
    grads(1)
    pass_on(2)
    second(0)
    second(1)
    grads(2)

    sp = r["sp"]

    def block(j, carry):
        sp[j % 2, j // 2] = sum(
            nn(r[f"expand{t}"][rows_at(j, quarter), :], r[f"grad{t}"][...]) for t in teachers
        ).astype(BF16)
        return carry

    lax.fori_loop(0, n_mp, block, 0)
    core_copy["s"] = send(sp.at[1 - core], r["sp_core"], (dp, sibling))
    third(0)
    second(2)
    third(1)
    core_copy["s"].wait_recv()
    sp[core, 1 - x] = (
        sp[core, 1 - x].astype(F32) + r["sp_core"][1 - x].astype(F32)
    ).astype(BF16)
    x_copy["s"] = send(sp.at[core, 1 - x], r["sp_x"], (dp, across))
    second(3)
    third(2)
    finish(0)
    own = sp[core, x].astype(F32) + r["sp_core"][x].astype(F32)
    x_copy["s"].wait_recv()
    summed = (own + r["sp_x"][...].astype(F32)).astype(BF16)
    placed = nt(r["sel"][...], summed).astype(BF16)
    r["home"][...] = placed.reshape(r["home"].shape)
    returns = [
        send(r["home"].at[peer], r["student_out"].at[dp], (peer, mp)) for peer in dp_peers
    ]
    r["student_out"][dp] = r["home"][dp]
    second(4)
    third(3)
    finish(1)
    second(5)
    third(4)
    finish(2)
    third(5)
    finish(3)
    finish(4)
    finish(5)
    for copy in returns:
        copy.wait_recv()
    for copy in sent:
        copy.wait_send()


def fused(
    student,
    dino_target,
    siglip_target,
    clip_target,
    image_owner,
    patch_count,
    dino_expand,
    dino_project,
    siglip_expand,
    siglip_project,
    clip_expand,
    clip_project,
):
    stores, groups = lax.axis_size("dp"), lax.axis_size("mp")
    mp = lax.axis_index("mp")
    per_store, patches = dino_target.shape[0], dino_target.shape[1]
    capacity = student.shape[0] // stores
    width = student.shape[2]
    quarter = width // groups
    rows = per_store * patches
    hidden = dino_expand.shape[1]
    xs = lax.dynamic_slice_in_dim(
        student.reshape(stores, capacity * patches, width), mp * quarter, quarter, axis=2
    )
    expands = (clip_expand, siglip_expand, dino_expand)
    projects = (clip_project, siglip_project, dino_project)
    targets = (clip_target, siglip_target, dino_target)

    inputs = {
        "xs": xs,
        "owners": image_owner.reshape(1, -1),
        "counts": patch_count.reshape(1, -1),
    }
    loaded = {}
    outputs = {"student_out": jax.ShapeDtypeStruct(xs.shape, BF16)}
    scratch = {
        "ssem": pltpu.SemaphoreType.DMA((52,)),
        "rsem": pltpu.SemaphoreType.DMA((52,)),
        "lsem": pltpu.SemaphoreType.DMA((9,)),
        "valid": pltpu.VMEM((1, rows), F32),
        "scale": pltpu.VMEM((1, hidden), F32),
        "xr": pltpu.VMEM(xs.shape, BF16),
        "home": pltpu.VMEM(xs.shape, BF16),
        "xt": pltpu.VMEM((width, rows), BF16),
        "sel": pltpu.VMEM((stores * capacity * patches, rows), BF16),
        "sp": pltpu.VMEM((2, 2, quarter, rows), BF16),
        "sp_core": pltpu.VMEM((2, quarter, rows), BF16),
        "sp_x": pltpu.VMEM((quarter, rows), BF16),
    }
    orders = []
    for t, (target, expand, project) in enumerate(zip(targets, expands, projects)):
        columns = target.shape[2]
        features = project.shape[1]
        loaded[f"expand{t}"] = expand
        loaded[f"project{t}"] = project
        loaded[f"target{t}"] = target.reshape(rows, columns)
        scratch[f"expand_t{t}"] = pltpu.VMEM(expand.shape[::-1], BF16)
        scratch[f"project_t{t}"] = pltpu.VMEM(project.shape[::-1], BF16)
        scratch[f"target_t{t}"] = pltpu.VMEM((columns, rows), BF16)
        scratch[f"slope{t}"] = pltpu.VMEM((hidden, rows), F32)
        scratch[f"act{t}"] = pltpu.VMEM((hidden, rows), BF16)
        scratch[f"grad{t}"] = pltpu.VMEM((hidden, rows), BF16)
        scratch[f"part{t}"] = pltpu.VMEM((2, 2, columns, rows), BF16)
        scratch[f"from_core{t}"] = pltpu.VMEM((2, columns, rows), BF16)
        scratch[f"from_x{t}"] = pltpu.VMEM((columns, rows), BF16)
        scratch[f"res{t}"] = pltpu.VMEM((features, rows), BF16)
        for i, size in ((2 * t, features // stores), (2 * t + 1, width // stores)):
            shape = (hidden, size) if i % 2 == 0 else (size, hidden)
            outputs[f"out{i}"] = jax.ShapeDtypeStruct(shape, F32)
            scratch[f"sum{i}"] = pltpu.VMEM((2, 2, 2, size, hidden), BF16)
            scratch[f"first{i}"] = pltpu.VMEM((2, 2, size, hidden), BF16)
            scratch[f"next{i}"] = pltpu.VMEM((2, size, hidden), BF16)
            scratch[f"last{i}"] = pltpu.VMEM((size, hidden), BF16)
            orders.append((2, 1, 4) if i in (0, 5) else (1, 2, 4))
    for name, value in loaded.items():
        scratch[name] = pltpu.VMEM(value.shape, BF16)
    held = [name + "_hbm" for name in loaded]
    names = list(inputs) + held + list(outputs) + list(scratch)
    vmem = pl.BlockSpec(memory_space=pltpu.VMEM)
    features = sum(project.shape[1] for project in projects)
    results = pl.pallas_call(
        functools.partial(fused_kernel, names, list(loaded), orders, capacity, patches),
        out_shape=tuple(outputs.values()),
        in_specs=[vmem] * len(inputs) + [pl.BlockSpec(memory_space=pl.ANY)] * len(loaded),
        out_specs=tuple([vmem] * len(outputs)),
        scratch_shapes=list(scratch.values()),
        compiler_params=pltpu.CompilerParams(
            collective_id=0, has_side_effects=True, vmem_limit_bytes=60 * 1024 * 1024
        ),
        cost_estimate=pl.CostEstimate(
            flops=6 * rows * hidden * (features + 3 * width),
            bytes_accessed=16 * 1024 * 1024,
            transcendentals=6 * rows * hidden,
        ),
    )(*inputs.values(), *loaded.values())
    student_grad = results[0].reshape(student.shape[0], patches, quarter)
    return (
        student_grad,
        results[6],
        results[5],
        results[4],
        results[3],
        results[2],
        results[1],
    )


def kernel_fits(mesh):
    return mesh.shape["dp"] == 8 and mesh.shape["mp"] == 4


def solution(mesh):
    return jax.shard_map(
        fused if kernel_fits(mesh) else shards,
        mesh=mesh,
        in_specs=(
            P("dp", None, None),
            P("dp", None, "mp"),
            P("dp", None, "mp"),
            P("dp", None, "mp"),
            P(),
            P(),
            P(None, "mp"),
            P("mp", None),
            P(None, "mp"),
            P("mp", None),
            P(None, "mp"),
            P("mp", None),
        ),
        out_specs=(
            P("dp", None, "mp"),
            P("dp", "mp"),
            P("mp", "dp"),
            P("dp", "mp"),
            P("mp", "dp"),
            P("dp", "mp"),
            P("mp", "dp"),
        ),
        check_vma=False,
    )
```

```python
import functools

import jax
import jax.numpy as jnp
from jax import lax
from jax.experimental import pallas as pl
from jax.experimental.pallas import tpu as pltpu
from jax.sharding import PartitionSpec as P

MESH = pl.DeviceIdType.MESH
F32 = jnp.float32
BF16 = jnp.bfloat16


def for_sending(value):

    def short(part):
        return part.astype(jnp.bfloat16) if part.dtype == jnp.float32 else part

    return jax.tree.map(short, value)


def gelu_parts(hidden):
    normal_cdf = 0.5 * (1.0 + jax.scipy.special.erf(hidden * 0.7071067811865476))
    density = jnp.exp(-0.5 * hidden * hidden) * 0.3989422804014327
    return (hidden * normal_cdf, normal_cdf + hidden * density)


def selection(store_block, owner_ids, capacity):
    belongs = (owner_ids[:, None] == store_block[None, :]).astype(jnp.int32)
    position = jnp.cumsum(belongs, axis=1) - 1
    ranks = jnp.arange(capacity, dtype=jnp.int32)
    return belongs[:, None, :] * (position[:, None, :] == ranks[None, :, None]).astype(jnp.int32)


def fold_step(activated, project, segment):
    back_sum = lax.dot_general(
        segment, project, (((1,), (1,)), ((), ())), preferred_element_type=jnp.float32
    )
    update = lax.dot_general(
        activated, segment, (((0,), (0,)), ((), ())), preferred_element_type=jnp.float32
    )
    return (back_sum, update)


def first_term(inputs, hidden_grad, loss_scale):
    return (
        lax.dot_general(
            inputs, hidden_grad, (((0,), (0,)), ((), ())), preferred_element_type=jnp.float32
        )
        * loss_scale
    )


def adapt(inputs, targets, slot_counts, weights, loss_scale):
    positions = jnp.arange(targets[0].shape[2], dtype=jnp.int32)
    valid_mask = (
        (positions[None, None, :] < slot_counts[:, :, None]).astype(jnp.float32).reshape(-1)
    )
    student_part = jnp.zeros(inputs.shape, jnp.float32)
    results = []
    for target, weight_pair in zip(targets, weights):
        expand, project = weight_pair
        hidden = jnp.dot(inputs, expand, preferred_element_type=jnp.float32)
        activated, gelu_slope = gelu_parts(hidden)
        activated = activated.astype(jnp.bfloat16)
        adapted = lax.psum_scatter(
            jnp.dot(activated, project, preferred_element_type=jnp.float32).astype(jnp.bfloat16),
            "mp",
            scatter_dimension=1,
            tiled=True,
        ).astype(jnp.float32)
        target_flat = target.reshape(-1, target.shape[3]).astype(jnp.float32)
        residual = ((adapted - target_flat) * valid_mask[:, None]).astype(jnp.bfloat16)
        back_sum, project_grad = fold_step(
            activated, project, lax.all_gather(residual, "mp", axis=1, tiled=True)
        )
        hidden_grad = (back_sum * gelu_slope).astype(jnp.bfloat16)
        expand_grad = lax.psum_scatter(
            first_term(inputs, hidden_grad, loss_scale).astype(jnp.bfloat16),
            "dp",
            scatter_dimension=0,
            tiled=True,
        ).astype(jnp.float32)
        project_grad = lax.psum_scatter(
            (project_grad * loss_scale).astype(jnp.bfloat16), "dp", scatter_dimension=1, tiled=True
        ).astype(jnp.float32)
        student_part = student_part + lax.dot_general(
            hidden_grad, expand, (((1,), (1,)), ((), ())), preferred_element_type=jnp.float32
        )
        results.append(expand_grad)
        results.append(project_grad)
    return (student_part, results)


def shards(
    student,
    dino_target,
    siglip_target,
    clip_target,
    image_owner,
    patch_count,
    dino_expand,
    dino_project,
    siglip_expand,
    siglip_project,
    clip_expand,
    clip_project,
):
    stores = lax.axis_size("dp")
    store_index = lax.axis_index("dp")
    per_store = dino_target.shape[0]
    patches = dino_target.shape[1]
    slot_total = student.shape[0]
    capacity = slot_total // stores
    owners = image_owner[:, 0]
    store_owner = owners.reshape(stores, per_store)
    counts_store = patch_count.reshape(stores, per_store)
    loss_scale = 1.0 / jnp.sqrt(jnp.sum(patch_count).astype(jnp.float32))
    own_block = lax.dynamic_slice_in_dim(owners, store_index * per_store, per_store)
    sel_store = selection(own_block, jnp.arange(stores, dtype=jnp.int32), capacity)
    picker = sel_store.astype(jnp.bfloat16)
    teachers = (dino_target, siglip_target, clip_target)
    weights = (
        (dino_expand, dino_project),
        (siglip_expand, siglip_project),
        (clip_expand, clip_project),
    )
    outgoing = tuple(
        (
            jnp.einsum("oki,ipf->okpf", picker, teacher, preferred_element_type=jnp.float32).astype(
                jnp.bfloat16
            )
            for teacher in teachers
        )
    )
    targets = jax.tree.map(
        lambda part, own: part.astype(own.dtype),
        lax.all_to_all(for_sending(outgoing), "dp", split_axis=0, concat_axis=0, tiled=True),
        outgoing,
    )
    owner_key = jnp.reshape(store_index, (1,))
    sel_owner = jax.vmap(lambda store_block: selection(store_block, owner_key, capacity)[0])(
        store_owner
    )
    slot_counts = jnp.sum(sel_owner * counts_store[:, None, :], axis=2)
    inputs = student.reshape(-1, student.shape[2])
    student_part, results = adapt(inputs, targets, slot_counts, weights, loss_scale)
    student_grad = lax.psum_scatter(
        student_part.reshape(slot_total, patches, -1).astype(jnp.bfloat16),
        "mp",
        scatter_dimension=2,
        tiled=True,
    )
    return (student_grad, results[0], results[1], results[2], results[3], results[4], results[5])


def nn(a, b):
    return lax.dot_general(a, b, (((1,), (0,)), ((), ())), preferred_element_type=F32)


def nt(a, b):
    return lax.dot_general(a, b, (((1,), (1,)), ((), ())), preferred_element_type=F32)


def tn(a, b):
    return lax.dot_general(a, b, (((0,), (0,)), ((), ())), preferred_element_type=F32)


def rows_at(index, size):
    return pl.ds(pl.multiple_of(index * size, 16), size)


def fused_kernel(names, names_loaded, orders, capacity, patches, *refs):
    r = dict(zip(names, refs))
    dp, mp = lax.axis_index("dp"), lax.axis_index("mp")
    x, core = mp // 2, mp % 2
    sibling = mp + 1 - 2 * core
    across = mp + 2 - 4 * x
    n_dp, n_mp = 8, 4
    sent = []
    numbers = iter(range(r["ssem"].shape[0]))

    def send(source, landing, device):
        number = next(numbers)
        copy = pltpu.make_async_remote_copy(
            src_ref=source,
            dst_ref=landing,
            send_sem=r["ssem"].at[number],
            recv_sem=r["rsem"].at[number],
            device_id=device,
            device_id_type=MESH,
        )
        copy.start()
        sent.append(copy)
        return copy

    loads = {}
    for number, name in enumerate(names_loaded):
        loads[name] = pltpu.make_async_copy(r[name + "_hbm"], r[name], r["lsem"].at[number])
        loads[name].start()

    dp_peers = [lax.rem(dp + k, n_dp) for k in range(1, n_dp)]
    barrier = pltpu.get_barrier_semaphore()
    for peer in dp_peers:
        pl.semaphore_signal(barrier, inc=1, device_id=(peer, mp), device_id_type=MESH)
    for peer in (sibling, across):
        pl.semaphore_signal(barrier, inc=1, device_id=(dp, peer), device_id_type=MESH)
    pl.semaphore_wait(barrier, n_dp + 1)

    xs, xr, xt = r["xs"], r["xr"], r["xt"]
    quarter = xt.shape[0] // n_mp
    slot_rows, row_total = xr.shape[0] * xr.shape[1], xt.shape[1]
    arrivals = [send(xs.at[peer], xr.at[dp], (peer, mp)) for peer in dp_peers]
    xr[dp] = xs[dp]

    owners, counts = r["owners"][...], r["counts"][...]
    images = owners.shape[1]
    per_store = row_total // patches
    first_image = dp * per_store
    image = lax.broadcasted_iota(jnp.int32, (images, row_total), 0) - first_image
    column = lax.broadcasted_iota(jnp.int32, (images, row_total), 1)
    at_column = column // patches
    same = (image == at_column).astype(F32).astype(BF16)
    before = ((image >= 0) & (image < at_column)).astype(F32).astype(BF16)
    padded = jnp.broadcast_to(owners, (8, images))
    owner_of = nn(padded.astype(F32).astype(BF16), same)
    count_of = nn(jnp.broadcast_to(counts, (8, images)).astype(F32).astype(BF16), same)
    named = lax.broadcasted_iota(jnp.int32, (n_dp, images), 0) == padded
    ranks = nn(named.astype(F32).astype(BF16), before)
    ours = lax.broadcasted_iota(jnp.int32, (n_dp, row_total), 0) == owner_of.astype(jnp.int32)
    rank = jnp.sum(jnp.where(ours, ranks, 0.0), axis=0, keepdims=True)
    patch = column[:1] - at_column[:1] * patches
    slot = owner_of[:1].astype(jnp.int32) * capacity + rank.astype(jnp.int32)
    r["valid"][...] = (patch < count_of[:1].astype(jnp.int32)).astype(F32)
    total = jnp.sum(counts.astype(F32), axis=1, keepdims=True)
    r["scale"][...] = jnp.broadcast_to(1.0 / jnp.sqrt(total), r["scale"].shape)
    place = slot * patches + patch
    picked = lax.broadcasted_iota(jnp.int32, (slot_rows, row_total), 0) == place
    r["sel"][...] = picked.astype(F32).astype(BF16)

    def turn(t):
        for kind in ("expand", "project", "target"):
            loads[f"{kind}{t}"].wait()
            r[f"{kind}_t{t}"][...] = r[f"{kind}{t}"][...].T

    turn(0)
    for copy in arrivals:
        copy.wait_recv()
    mine = rows_at(mp, quarter)
    theirs = rows_at(across, quarter)
    xt[mine, :] = tn(xr[...].reshape(slot_rows, quarter), r["sel"][...]).astype(BF16)
    to_sibling = send(xt.at[mine, :], xt.at[mine, :], (dp, sibling))
    to_across = send(xt.at[mine, :], xt.at[mine, :], (dp, across))
    turn(1)
    to_across.wait_recv()
    forward = send(xt.at[theirs, :], xt.at[theirs, :], (dp, sibling))
    to_sibling.wait_recv()
    forward.wait_recv()

    teachers = range(3)
    core_copy, x_copy, gather = {}, {}, {}

    def first_half(t):
        project_t = r[f"project_t{t}"]
        hidden = nn(r[f"expand_t{t}"][...], xt[...])
        cdf = 0.5 * (1.0 + lax.erf(hidden * 0.7071067811865476))
        density = jnp.exp(-0.5 * hidden * hidden) * 0.3989422804014327
        r[f"slope{t}"][...] = cdf + hidden * density
        r[f"act{t}"][...] = (hidden * cdf).astype(BF16)
        part = r[f"part{t}"]
        width = part.shape[2]

        def block(j, carry):
            part[j % 2, j // 2] = nn(
                project_t[rows_at(j, width), :], r[f"act{t}"][...]
            ).astype(BF16)
            return carry

        lax.fori_loop(0, n_mp, block, 0)
        core_copy[t] = send(part.at[1 - core], r[f"from_core{t}"], (dp, sibling))

    def to_x(t):
        part, landed = r[f"part{t}"], r[f"from_core{t}"]
        core_copy[t].wait_recv()
        part[core, 1 - x] = (
            part[core, 1 - x].astype(F32) + landed[1 - x].astype(F32)
        ).astype(BF16)
        x_copy[t] = send(part.at[core, 1 - x], r[f"from_x{t}"], (dp, across))

    def residual(t):
        part, landed, res = r[f"part{t}"], r[f"from_core{t}"], r[f"res{t}"]
        width = part.shape[2]
        own = part[core, x].astype(F32) + landed[x].astype(F32)
        x_copy[t].wait_recv()
        adapted = own + r[f"from_x{t}"][...].astype(F32)
        here = rows_at(mp, width)
        res[here, :] = ((adapted - r[f"target_t{t}"][...].astype(F32)) * r["valid"][...]).astype(BF16)
        near = send(res.at[here, :], res.at[here, :], (dp, sibling))
        far = send(res.at[here, :], res.at[here, :], (dp, across))
        gather[t] = (near, far)

    def pass_on(t):
        res = r[f"res{t}"]
        there = rows_at(across, r[f"part{t}"].shape[2])
        near, far = gather[t]
        far.wait_recv()
        gather[t] = (near, send(res.at[there, :], res.at[there, :], (dp, sibling)))

    def bit_of(index, bit):
        return (index // bit) % 2

    def partner(bit):
        return dp + bit - 2 * bit * bit_of(dp, bit)

    stage = {}

    def start_reduce(i):
        total, order = r[f"sum{i}"], orders[i]
        stage[i] = send(
            total.at[1 - bit_of(dp, order[0])], r[f"first{i}"], (partner(order[0]), mp)
        )

    def second(i):
        total, landed, order = r[f"sum{i}"], r[f"first{i}"], orders[i]
        own = bit_of(dp, order[0])
        stage[i].wait_recv()

        def block(k, carry):
            a, b = k // 2, k % 2
            total[own, a, b] = total[own, a, b] + landed[a, b]
            return carry

        lax.fori_loop(0, 4, block, 0)
        stage[i] = send(
            total.at[own, 1 - bit_of(dp, order[1])], r[f"next{i}"], (partner(order[1]), mp)
        )

    def third(i):
        total, landed, order = r[f"sum{i}"], r[f"next{i}"], orders[i]
        own, mid = bit_of(dp, order[0]), bit_of(dp, order[1])
        stage[i].wait_recv()

        def block(k, carry):
            total[own, mid, k] = total[own, mid, k] + landed[k]
            return carry

        lax.fori_loop(0, 2, block, 0)
        stage[i] = send(
            total.at[own, mid, 1 - bit_of(dp, order[2])], r[f"last{i}"], (partner(order[2]), mp)
        )

    def finish(i):
        total, order = r[f"sum{i}"], orders[i]
        own = [bit_of(dp, bit) for bit in order]
        stage[i].wait_recv()
        summed = (
            total[own[0], own[1], own[2]].astype(F32) + r[f"last{i}"][...].astype(F32)
        ) * r["scale"][...]
        r[f"out{i}"][...] = summed.T if i == 0 else summed

    def weight_grad(i, left, right):
        total, order = r[f"sum{i}"], orders[i]
        size = total.shape[3]

        def block(k, carry):
            both = nt(left[rows_at(k, 2 * size), :], right[...]).astype(BF16)
            for low in (0, 1):
                at = [bit_of(2 * k + low, bit) for bit in order]
                total[at[0], at[1], at[2]] = both[low * size : (low + 1) * size]
            return carry

        lax.fori_loop(0, n_dp // 2, block, 0)

    def project_grad(t):
        near, forwarded = gather[t]
        near.wait_recv()
        forwarded.wait_recv()
        weight_grad(2 * t, r[f"res{t}"], r[f"act{t}"])
        start_reduce(2 * t)

    def hidden_grad(t):
        back = nn(r[f"project{t}"][...], r[f"res{t}"][...])
        r[f"grad{t}"][...] = (back * r[f"slope{t}"][...]).astype(BF16)

    def expand_grad(t):
        weight_grad(2 * t + 1, xt, r[f"grad{t}"])

    first_half(0)
    to_x(0)
    first_half(1)
    residual(0)
    turn(2)
    first_half(2)
    pass_on(0)
    to_x(1)
    project_grad(0)
    hidden_grad(0)
    expand_grad(0)
    start_reduce(1)
    residual(1)
    second(0)
    pass_on(1)
    to_x(2)
    project_grad(1)
    hidden_grad(1)
    expand_grad(1)
    second(1)
    third(0)
    residual(2)
    second(2)
    start_reduce(3)
    pass_on(2)
    project_grad(2)
    hidden_grad(2)

    sp = r["sp"]

    def block(j, carry):
        sp[j % 2, j // 2] = sum(
            nn(r[f"expand{t}"][rows_at(j, quarter), :], r[f"grad{t}"][...]) for t in teachers
        ).astype(BF16)
        return carry

    lax.fori_loop(0, n_mp, block, 0)
    core_copy["s"] = send(sp.at[1 - core], r["sp_core"], (dp, sibling))
    expand_grad(2)
    start_reduce(5)
    core_copy["s"].wait_recv()
    sp[core, 1 - x] = (
        sp[core, 1 - x].astype(F32) + r["sp_core"][1 - x].astype(F32)
    ).astype(BF16)
    x_copy["s"] = send(sp.at[core, 1 - x], r["sp_x"], (dp, across))
    third(1)
    second(3)
    third(2)
    finish(0)
    own = sp[core, x].astype(F32) + r["sp_core"][x].astype(F32)
    x_copy["s"].wait_recv()
    summed = (own + r["sp_x"][...].astype(F32)).astype(BF16)
    placed = nt(r["sel"][...], summed).astype(BF16)
    r["home"][...] = placed.reshape(r["home"].shape)
    returns = [
        send(r["home"].at[peer], r["student_out"].at[dp], (peer, mp)) for peer in dp_peers
    ]
    r["student_out"][dp] = r["home"][dp]
    finish(1)
    third(3)
    second(5)
    finish(2)
    second(4)
    finish(3)
    third(5)
    third(4)
    finish(5)
    finish(4)
    for copy in returns:
        copy.wait_recv()
    for copy in sent:
        copy.wait_send()


def copy_kernel(*refs):
    count = len(refs) // 2
    copies = [
        pltpu.make_async_copy(refs[i], refs[count + i], refs[-1].at[i]) for i in range(count)
    ]
    for copy in copies:
        copy.start()
    for copy in copies:
        copy.wait()


def fused(
    student,
    dino_target,
    siglip_target,
    clip_target,
    image_owner,
    patch_count,
    dino_expand,
    dino_project,
    siglip_expand,
    siglip_project,
    clip_expand,
    clip_project,
):
    stores, groups = lax.axis_size("dp"), lax.axis_size("mp")
    mp = lax.axis_index("mp")
    per_store, patches = dino_target.shape[0], dino_target.shape[1]
    capacity = student.shape[0] // stores
    width = student.shape[2]
    quarter = width // groups
    rows = per_store * patches
    hidden = dino_expand.shape[1]
    xs = lax.dynamic_slice_in_dim(
        student.reshape(stores, capacity * patches, width), mp * quarter, quarter, axis=2
    )
    expands = (clip_expand, siglip_expand, dino_expand)
    projects = (clip_project, siglip_project, dino_project)
    targets = (clip_target, siglip_target, dino_target)

    inputs = {
        "xs": xs,
        "owners": image_owner.reshape(1, -1),
        "counts": patch_count.reshape(1, -1),
    }
    loaded = {}
    outputs = {"student_out": jax.ShapeDtypeStruct(xs.shape, BF16)}
    scratch = {
        "ssem": pltpu.SemaphoreType.DMA((52,)),
        "rsem": pltpu.SemaphoreType.DMA((52,)),
        "lsem": pltpu.SemaphoreType.DMA((9,)),
        "valid": pltpu.VMEM((1, rows), F32),
        "scale": pltpu.VMEM((1, hidden), F32),
        "xr": pltpu.VMEM(xs.shape, BF16),
        "home": pltpu.VMEM(xs.shape, BF16),
        "xt": pltpu.VMEM((width, rows), BF16),
        "sel": pltpu.VMEM((stores * capacity * patches, rows), BF16),
        "sp": pltpu.VMEM((2, 2, quarter, rows), BF16),
        "sp_core": pltpu.VMEM((2, quarter, rows), BF16),
        "sp_x": pltpu.VMEM((quarter, rows), BF16),
    }
    orders = []
    for t, (target, expand, project) in enumerate(zip(targets, expands, projects)):
        columns = target.shape[2]
        features = project.shape[1]
        loaded[f"expand{t}"] = expand
        loaded[f"project{t}"] = project
        loaded[f"target{t}"] = target.reshape(rows, columns)
        scratch[f"expand_t{t}"] = pltpu.VMEM(expand.shape[::-1], BF16)
        scratch[f"project_t{t}"] = pltpu.VMEM(project.shape[::-1], BF16)
        scratch[f"target_t{t}"] = pltpu.VMEM((columns, rows), BF16)
        scratch[f"slope{t}"] = pltpu.VMEM((hidden, rows), F32)
        scratch[f"act{t}"] = pltpu.VMEM((hidden, rows), BF16)
        scratch[f"grad{t}"] = pltpu.VMEM((hidden, rows), BF16)
        scratch[f"part{t}"] = pltpu.VMEM((2, 2, columns, rows), BF16)
        scratch[f"from_core{t}"] = pltpu.VMEM((2, columns, rows), BF16)
        scratch[f"from_x{t}"] = pltpu.VMEM((columns, rows), BF16)
        scratch[f"res{t}"] = pltpu.VMEM((features, rows), BF16)
        for i, size in ((2 * t, features // stores), (2 * t + 1, width // stores)):
            shape = (hidden, size) if i == 0 else (size, hidden)
            outputs[f"out{i}"] = jax.ShapeDtypeStruct(shape, F32)
            scratch[f"sum{i}"] = pltpu.VMEM((2, 2, 2, size, hidden), BF16)
            scratch[f"first{i}"] = pltpu.VMEM((2, 2, size, hidden), BF16)
            scratch[f"next{i}"] = pltpu.VMEM((2, size, hidden), BF16)
            scratch[f"last{i}"] = pltpu.VMEM((size, hidden), BF16)
            orders.append((2, 1, 4) if i in (0, 5) else (1, 2, 4))
    for name, value in loaded.items():
        scratch[name] = pltpu.VMEM(value.shape, BF16)
    held = [name + "_hbm" for name in loaded]
    names = list(inputs) + held + list(outputs) + list(scratch)
    vmem = pl.BlockSpec(memory_space=pltpu.VMEM)
    features = sum(project.shape[1] for project in projects)
    results = pl.pallas_call(
        functools.partial(fused_kernel, names, list(loaded), orders, capacity, patches),
        out_shape=tuple(outputs.values()),
        in_specs=[vmem] * len(inputs) + [pl.BlockSpec(memory_space=pltpu.HBM)] * len(loaded),
        out_specs=tuple([vmem] * len(outputs)),
        scratch_shapes=list(scratch.values()),
        compiler_params=pltpu.CompilerParams(
            collective_id=0, has_side_effects=True, vmem_limit_bytes=60 * 1024 * 1024
        ),
        cost_estimate=pl.CostEstimate(
            flops=6 * rows * hidden * (features + 3 * width),
            bytes_accessed=16 * 1024 * 1024,
            transcendentals=6 * rows * hidden,
        ),
    )(*inputs.values(), *loaded.values())
    anywhere = pl.BlockSpec(memory_space=pltpu.HBM)
    results = pl.pallas_call(
        copy_kernel,
        out_shape=tuple(outputs.values()),
        in_specs=[anywhere] * len(outputs),
        out_specs=tuple([anywhere] * len(outputs)),
        scratch_shapes=[pltpu.SemaphoreType.DMA((len(outputs),))],
        compiler_params=pltpu.CompilerParams(vmem_limit_bytes=60 * 1024 * 1024),
    )(*results)
    student_grad = results[0].reshape(student.shape[0], patches, quarter)
    return (
        student_grad,
        results[6],
        results[5].T,
        results[4],
        results[3].T,
        results[2],
        results[1],
    )


def kernel_fits(mesh):
    return mesh.shape["dp"] == 8 and mesh.shape["mp"] == 4


def solution(mesh):
    return jax.shard_map(
        fused if kernel_fits(mesh) else shards,
        mesh=mesh,
        in_specs=(
            P("dp", None, None),
            P("dp", None, "mp"),
            P("dp", None, "mp"),
            P("dp", None, "mp"),
            P(),
            P(),
            P(None, "mp"),
            P("mp", None),
            P(None, "mp"),
            P("mp", None),
            P(None, "mp"),
            P("mp", None),
        ),
        out_specs=(
            P("dp", None, "mp"),
            P("dp", "mp"),
            P("mp", "dp"),
            P("dp", "mp"),
            P("mp", "dp"),
            P("dp", "mp"),
            P("mp", "dp"),
        ),
        check_vma=False,
    )
```

```python
import functools

import jax
import jax.numpy as jnp
from jax import lax
from jax.experimental import pallas as pl
from jax.experimental.pallas import tpu as pltpu
from jax.sharding import PartitionSpec as P

MESH = pl.DeviceIdType.MESH
F32 = jnp.float32
BF16 = jnp.bfloat16


def for_sending(value):

    def short(part):
        return part.astype(jnp.bfloat16) if part.dtype == jnp.float32 else part

    return jax.tree.map(short, value)


def gelu_parts(hidden):
    normal_cdf = 0.5 * (1.0 + jax.scipy.special.erf(hidden * 0.7071067811865476))
    density = jnp.exp(-0.5 * hidden * hidden) * 0.3989422804014327
    return (hidden * normal_cdf, normal_cdf + hidden * density)


def selection(store_block, owner_ids, capacity):
    belongs = (owner_ids[:, None] == store_block[None, :]).astype(jnp.int32)
    position = jnp.cumsum(belongs, axis=1) - 1
    ranks = jnp.arange(capacity, dtype=jnp.int32)
    return belongs[:, None, :] * (position[:, None, :] == ranks[None, :, None]).astype(jnp.int32)


def fold_step(activated, project, segment):
    back_sum = lax.dot_general(
        segment, project, (((1,), (1,)), ((), ())), preferred_element_type=jnp.float32
    )
    update = lax.dot_general(
        activated, segment, (((0,), (0,)), ((), ())), preferred_element_type=jnp.float32
    )
    return (back_sum, update)


def first_term(inputs, hidden_grad, loss_scale):
    return (
        lax.dot_general(
            inputs, hidden_grad, (((0,), (0,)), ((), ())), preferred_element_type=jnp.float32
        )
        * loss_scale
    )


def adapt(inputs, targets, slot_counts, weights, loss_scale):
    positions = jnp.arange(targets[0].shape[2], dtype=jnp.int32)
    valid_mask = (
        (positions[None, None, :] < slot_counts[:, :, None]).astype(jnp.float32).reshape(-1)
    )
    student_part = jnp.zeros(inputs.shape, jnp.float32)
    results = []
    for target, weight_pair in zip(targets, weights):
        expand, project = weight_pair
        hidden = jnp.dot(inputs, expand, preferred_element_type=jnp.float32)
        activated, gelu_slope = gelu_parts(hidden)
        activated = activated.astype(jnp.bfloat16)
        adapted = lax.psum_scatter(
            jnp.dot(activated, project, preferred_element_type=jnp.float32).astype(jnp.bfloat16),
            "mp",
            scatter_dimension=1,
            tiled=True,
        ).astype(jnp.float32)
        target_flat = target.reshape(-1, target.shape[3]).astype(jnp.float32)
        residual = ((adapted - target_flat) * valid_mask[:, None]).astype(jnp.bfloat16)
        back_sum, project_grad = fold_step(
            activated, project, lax.all_gather(residual, "mp", axis=1, tiled=True)
        )
        hidden_grad = (back_sum * gelu_slope).astype(jnp.bfloat16)
        expand_grad = lax.psum_scatter(
            first_term(inputs, hidden_grad, loss_scale).astype(jnp.bfloat16),
            "dp",
            scatter_dimension=0,
            tiled=True,
        ).astype(jnp.float32)
        project_grad = lax.psum_scatter(
            (project_grad * loss_scale).astype(jnp.bfloat16), "dp", scatter_dimension=1, tiled=True
        ).astype(jnp.float32)
        student_part = student_part + lax.dot_general(
            hidden_grad, expand, (((1,), (1,)), ((), ())), preferred_element_type=jnp.float32
        )
        results.append(expand_grad)
        results.append(project_grad)
    return (student_part, results)


def shards(
    student,
    dino_target,
    siglip_target,
    clip_target,
    image_owner,
    patch_count,
    dino_expand,
    dino_project,
    siglip_expand,
    siglip_project,
    clip_expand,
    clip_project,
):
    stores = lax.axis_size("dp")
    store_index = lax.axis_index("dp")
    per_store = dino_target.shape[0]
    patches = dino_target.shape[1]
    slot_total = student.shape[0]
    capacity = slot_total // stores
    owners = image_owner[:, 0]
    store_owner = owners.reshape(stores, per_store)
    counts_store = patch_count.reshape(stores, per_store)
    loss_scale = 1.0 / jnp.sqrt(jnp.sum(patch_count).astype(jnp.float32))
    own_block = lax.dynamic_slice_in_dim(owners, store_index * per_store, per_store)
    sel_store = selection(own_block, jnp.arange(stores, dtype=jnp.int32), capacity)
    picker = sel_store.astype(jnp.bfloat16)
    teachers = (dino_target, siglip_target, clip_target)
    weights = (
        (dino_expand, dino_project),
        (siglip_expand, siglip_project),
        (clip_expand, clip_project),
    )
    outgoing = tuple(
        (
            jnp.einsum("oki,ipf->okpf", picker, teacher, preferred_element_type=jnp.float32).astype(
                jnp.bfloat16
            )
            for teacher in teachers
        )
    )
    targets = jax.tree.map(
        lambda part, own: part.astype(own.dtype),
        lax.all_to_all(for_sending(outgoing), "dp", split_axis=0, concat_axis=0, tiled=True),
        outgoing,
    )
    owner_key = jnp.reshape(store_index, (1,))
    sel_owner = jax.vmap(lambda store_block: selection(store_block, owner_key, capacity)[0])(
        store_owner
    )
    slot_counts = jnp.sum(sel_owner * counts_store[:, None, :], axis=2)
    inputs = student.reshape(-1, student.shape[2])
    student_part, results = adapt(inputs, targets, slot_counts, weights, loss_scale)
    student_grad = lax.psum_scatter(
        student_part.reshape(slot_total, patches, -1).astype(jnp.bfloat16),
        "mp",
        scatter_dimension=2,
        tiled=True,
    )
    return (student_grad, results[0], results[1], results[2], results[3], results[4], results[5])


def nn(a, b):
    return lax.dot_general(a, b, (((1,), (0,)), ((), ())), preferred_element_type=F32)


def nt(a, b):
    return lax.dot_general(a, b, (((1,), (1,)), ((), ())), preferred_element_type=F32)


def tn(a, b):
    return lax.dot_general(a, b, (((0,), (0,)), ((), ())), preferred_element_type=F32)


def rows_at(index, size):
    return pl.ds(pl.multiple_of(index * size, 16), size)


def fused_kernel(names, names_loaded, orders, capacity, patches, *refs):
    r = dict(zip(names, refs))
    dp, mp = lax.axis_index("dp"), lax.axis_index("mp")
    x, core = mp // 2, mp % 2
    sibling = mp + 1 - 2 * core
    across = mp + 2 - 4 * x
    n_dp, n_mp = 8, 4
    sent = []
    numbers = iter(range(r["ssem"].shape[0]))

    def send(source, landing, device):
        number = next(numbers)
        copy = pltpu.make_async_remote_copy(
            src_ref=source,
            dst_ref=landing,
            send_sem=r["ssem"].at[number],
            recv_sem=r["rsem"].at[number],
            device_id=device,
            device_id_type=MESH,
        )
        copy.start()
        sent.append(copy)
        return copy

    loads = {}
    for number, name in enumerate(names_loaded):
        loads[name] = pltpu.make_async_copy(r[name + "_hbm"], r[name], r["lsem"].at[number])
        loads[name].start()

    dp_peers = [lax.rem(dp + k, n_dp) for k in range(1, n_dp)]
    barrier = pltpu.get_barrier_semaphore()
    for peer in dp_peers:
        pl.semaphore_signal(barrier, inc=1, device_id=(peer, mp), device_id_type=MESH)
    for peer in (sibling, across):
        pl.semaphore_signal(barrier, inc=1, device_id=(dp, peer), device_id_type=MESH)
    pl.semaphore_wait(barrier, n_dp + 1)

    xs, xr, xt = r["xs"], r["xr"], r["xt"]
    quarter = xt.shape[0] // n_mp
    slot_rows, row_total = xr.shape[0] * xr.shape[1], xt.shape[1]
    arrivals = [send(xs.at[peer], xr.at[dp], (peer, mp)) for peer in dp_peers]
    xr[dp] = xs[dp]

    owners, counts = r["owners"][...], r["counts"][...]
    images = owners.shape[1]
    per_store = row_total // patches
    first_image = dp * per_store
    image = lax.broadcasted_iota(jnp.int32, (images, row_total), 0) - first_image
    column = lax.broadcasted_iota(jnp.int32, (images, row_total), 1)
    at_column = column // patches
    same = (image == at_column).astype(F32).astype(BF16)
    before = ((image >= 0) & (image < at_column)).astype(F32).astype(BF16)
    padded = jnp.broadcast_to(owners, (8, images))
    owner_of = nn(padded.astype(F32).astype(BF16), same)
    count_of = nn(jnp.broadcast_to(counts, (8, images)).astype(F32).astype(BF16), same)
    named = lax.broadcasted_iota(jnp.int32, (n_dp, images), 0) == padded
    ranks = nn(named.astype(F32).astype(BF16), before)
    ours = lax.broadcasted_iota(jnp.int32, (n_dp, row_total), 0) == owner_of.astype(jnp.int32)
    rank = jnp.sum(jnp.where(ours, ranks, 0.0), axis=0, keepdims=True)
    patch = column[:1] - at_column[:1] * patches
    slot = owner_of[:1].astype(jnp.int32) * capacity + rank.astype(jnp.int32)
    r["valid"][...] = (patch < count_of[:1].astype(jnp.int32)).astype(F32)
    total = jnp.sum(counts.astype(F32), axis=1, keepdims=True)
    r["scale"][...] = jnp.broadcast_to(1.0 / jnp.sqrt(total), r["scale"].shape)
    place = slot * patches + patch
    picked = lax.broadcasted_iota(jnp.int32, (slot_rows, row_total), 0) == place
    r["sel"][...] = picked.astype(F32).astype(BF16)

    def turn(t):
        for kind in ("expand", "project", "target"):
            loads[f"{kind}{t}"].wait()
            r[f"{kind}_t{t}"][...] = r[f"{kind}{t}"][...].T

    turn(0)
    turn(1)
    for copy in arrivals:
        copy.wait_recv()
    mine = rows_at(mp, quarter)
    theirs = rows_at(across, quarter)
    xt[mine, :] = tn(xr[...].reshape(slot_rows, quarter), r["sel"][...]).astype(BF16)
    to_sibling = send(xt.at[mine, :], xt.at[mine, :], (dp, sibling))
    to_across = send(xt.at[mine, :], xt.at[mine, :], (dp, across))
    turn(2)
    to_across.wait_recv()
    forward = send(xt.at[theirs, :], xt.at[theirs, :], (dp, sibling))
    to_sibling.wait_recv()
    forward.wait_recv()

    teachers = range(3)
    core_copy, x_copy, gather = {}, {}, {}

    def first_half(t):
        project_t = r[f"project_t{t}"]
        hidden = nn(r[f"expand_t{t}"][...], xt[...])
        cdf = 0.5 * (1.0 + lax.erf(hidden * 0.7071067811865476))
        density = jnp.exp(-0.5 * hidden * hidden) * 0.3989422804014327
        r[f"slope{t}"][...] = cdf + hidden * density
        r[f"act{t}"][...] = (hidden * cdf).astype(BF16)
        part = r[f"part{t}"]
        width = part.shape[2]

        def block(j, carry):
            part[j % 2, j // 2] = nn(
                project_t[rows_at(j, width), :], r[f"act{t}"][...]
            ).astype(BF16)
            return carry

        lax.fori_loop(0, n_mp, block, 0)
        core_copy[t] = send(part.at[1 - core], r[f"from_core{t}"], (dp, sibling))

    def to_x(t):
        part, landed = r[f"part{t}"], r[f"from_core{t}"]
        core_copy[t].wait_recv()
        part[core, 1 - x] = (
            part[core, 1 - x].astype(F32) + landed[1 - x].astype(F32)
        ).astype(BF16)
        x_copy[t] = send(part.at[core, 1 - x], r[f"from_x{t}"], (dp, across))

    def residual(t):
        part, landed, res = r[f"part{t}"], r[f"from_core{t}"], r[f"res{t}"]
        width = part.shape[2]
        own = part[core, x].astype(F32) + landed[x].astype(F32)
        x_copy[t].wait_recv()
        adapted = own + r[f"from_x{t}"][...].astype(F32)
        here = rows_at(mp, width)
        res[here, :] = ((adapted - r[f"target_t{t}"][...].astype(F32)) * r["valid"][...]).astype(BF16)
        near = send(res.at[here, :], res.at[here, :], (dp, sibling))
        far = send(res.at[here, :], res.at[here, :], (dp, across))
        gather[t] = (near, far)

    def pass_on(t):
        res = r[f"res{t}"]
        there = rows_at(across, r[f"part{t}"].shape[2])
        near, far = gather[t]
        far.wait_recv()
        gather[t] = (near, send(res.at[there, :], res.at[there, :], (dp, sibling)))

    def bit_of(index, bit):
        return (index // bit) % 2

    def partner(bit):
        return dp + bit - 2 * bit * bit_of(dp, bit)

    stage = {}

    def start_reduce(i):
        total, order = r[f"sum{i}"], orders[i]
        stage[i] = send(
            total.at[1 - bit_of(dp, order[0])], r[f"first{i}"], (partner(order[0]), mp)
        )

    def second(i):
        total, landed, order = r[f"sum{i}"], r[f"first{i}"], orders[i]
        own = bit_of(dp, order[0])
        stage[i].wait_recv()

        def block(k, carry):
            a, b = k // 2, k % 2
            total[own, a, b] = total[own, a, b] + landed[a, b]
            return carry

        lax.fori_loop(0, 4, block, 0)
        stage[i] = send(
            total.at[own, 1 - bit_of(dp, order[1])], r[f"next{i}"], (partner(order[1]), mp)
        )

    def third(i):
        total, landed, order = r[f"sum{i}"], r[f"next{i}"], orders[i]
        own, mid = bit_of(dp, order[0]), bit_of(dp, order[1])
        stage[i].wait_recv()

        def block(k, carry):
            total[own, mid, k] = total[own, mid, k] + landed[k]
            return carry

        lax.fori_loop(0, 2, block, 0)
        stage[i] = send(
            total.at[own, mid, 1 - bit_of(dp, order[2])], r[f"last{i}"], (partner(order[2]), mp)
        )

    def finish(i):
        total, order = r[f"sum{i}"], orders[i]
        own = [bit_of(dp, bit) for bit in order]
        stage[i].wait_recv()
        summed = (
            total[own[0], own[1], own[2]].astype(F32) + r[f"last{i}"][...].astype(F32)
        ) * r["scale"][...]
        r[f"out{i}"][...] = summed.T if i == 0 else summed

    def weight_grad(i, left, right):
        total, order = r[f"sum{i}"], orders[i]
        size = total.shape[3]

        def block(k, carry):
            both = nt(left[rows_at(k, 2 * size), :], right[...]).astype(BF16)
            for low in (0, 1):
                at = [bit_of(2 * k + low, bit) for bit in order]
                total[at[0], at[1], at[2]] = both[low * size : (low + 1) * size]
            return carry

        lax.fori_loop(0, n_dp // 2, block, 0)

    def project_grad(t):
        near, forwarded = gather[t]
        near.wait_recv()
        forwarded.wait_recv()
        weight_grad(2 * t, r[f"res{t}"], r[f"act{t}"])
        start_reduce(2 * t)

    def hidden_grad(t):
        back = nn(r[f"project{t}"][...], r[f"res{t}"][...])
        r[f"grad{t}"][...] = (back * r[f"slope{t}"][...]).astype(BF16)

    def expand_grad(t):
        weight_grad(2 * t + 1, xt, r[f"grad{t}"])

    first_half(0)
    to_x(0)
    first_half(1)
    residual(0)
    to_x(1)
    first_half(2)
    pass_on(0)
    project_grad(0)
    residual(1)
    to_x(2)
    hidden_grad(0)
    expand_grad(0)
    start_reduce(1)
    pass_on(1)
    project_grad(1)
    hidden_grad(1)
    residual(2)
    expand_grad(1)
    start_reduce(3)
    second(0)
    pass_on(2)
    project_grad(2)
    hidden_grad(2)

    sp = r["sp"]

    def block(j, carry):
        sp[j % 2, j // 2] = sum(
            nn(r[f"expand{t}"][rows_at(j, quarter), :], r[f"grad{t}"][...]) for t in teachers
        ).astype(BF16)
        return carry

    lax.fori_loop(0, n_mp, block, 0)
    core_copy["s"] = send(sp.at[1 - core], r["sp_core"], (dp, sibling))
    expand_grad(2)
    start_reduce(5)
    second(1)
    third(0)
    core_copy["s"].wait_recv()
    sp[core, 1 - x] = (
        sp[core, 1 - x].astype(F32) + r["sp_core"][1 - x].astype(F32)
    ).astype(BF16)
    x_copy["s"] = send(sp.at[core, 1 - x], r["sp_x"], (dp, across))
    second(2)
    third(1)
    finish(0)
    own = sp[core, x].astype(F32) + r["sp_core"][x].astype(F32)
    x_copy["s"].wait_recv()
    summed = (own + r["sp_x"][...].astype(F32)).astype(BF16)
    placed = nt(r["sel"][...], summed).astype(BF16)
    r["home"][...] = placed.reshape(r["home"].shape)
    returns = [
        send(r["home"].at[peer], r["student_out"].at[dp], (peer, mp)) for peer in dp_peers
    ]
    r["student_out"][dp] = r["home"][dp]
    second(3)
    third(2)
    finish(1)
    second(5)
    third(3)
    finish(2)
    second(4)
    finish(3)
    third(5)
    third(4)
    finish(5)
    finish(4)
    for copy in returns:
        copy.wait_recv()
    for copy in sent:
        copy.wait_send()


def copy_kernel(*refs):
    count = len(refs) // 3
    sources, results, held = refs[:count], refs[count : 2 * count], refs[2 * count : 3 * count]
    entry, leave = refs[3 * count :]
    arrive = [pltpu.make_async_copy(sources[i], held[i], entry.at[i]) for i in range(count)]
    depart = [pltpu.make_async_copy(held[i], results[i], leave.at[i]) for i in range(count)]
    for copy in arrive:
        copy.start()
    for i in range(count):
        arrive[i].wait()
        depart[i].start()
    for copy in depart:
        copy.wait()


def fused(
    student,
    dino_target,
    siglip_target,
    clip_target,
    image_owner,
    patch_count,
    dino_expand,
    dino_project,
    siglip_expand,
    siglip_project,
    clip_expand,
    clip_project,
):
    stores, groups = lax.axis_size("dp"), lax.axis_size("mp")
    mp = lax.axis_index("mp")
    per_store, patches = dino_target.shape[0], dino_target.shape[1]
    capacity = student.shape[0] // stores
    width = student.shape[2]
    quarter = width // groups
    rows = per_store * patches
    hidden = dino_expand.shape[1]
    xs = lax.dynamic_slice_in_dim(
        student.reshape(stores, capacity * patches, width), mp * quarter, quarter, axis=2
    )
    expands = (clip_expand, siglip_expand, dino_expand)
    projects = (clip_project, siglip_project, dino_project)
    targets = (clip_target, siglip_target, dino_target)

    inputs = {
        "xs": xs,
        "owners": image_owner.reshape(1, -1),
        "counts": patch_count.reshape(1, -1),
    }
    loaded = {}
    outputs = {"student_out": jax.ShapeDtypeStruct(xs.shape, BF16)}
    scratch = {
        "ssem": pltpu.SemaphoreType.DMA((52,)),
        "rsem": pltpu.SemaphoreType.DMA((52,)),
        "lsem": pltpu.SemaphoreType.DMA((9,)),
        "valid": pltpu.VMEM((1, rows), F32),
        "scale": pltpu.VMEM((1, hidden), F32),
        "xr": pltpu.VMEM(xs.shape, BF16),
        "home": pltpu.VMEM(xs.shape, BF16),
        "xt": pltpu.VMEM((width, rows), BF16),
        "sel": pltpu.VMEM((stores * capacity * patches, rows), BF16),
        "sp": pltpu.VMEM((2, 2, quarter, rows), BF16),
        "sp_core": pltpu.VMEM((2, quarter, rows), BF16),
        "sp_x": pltpu.VMEM((quarter, rows), BF16),
    }
    orders = []
    for t, (target, expand, project) in enumerate(zip(targets, expands, projects)):
        columns = target.shape[2]
        features = project.shape[1]
        loaded[f"expand{t}"] = expand
        loaded[f"project{t}"] = project
        loaded[f"target{t}"] = target.reshape(rows, columns)
        scratch[f"expand_t{t}"] = pltpu.VMEM(expand.shape[::-1], BF16)
        scratch[f"project_t{t}"] = pltpu.VMEM(project.shape[::-1], BF16)
        scratch[f"target_t{t}"] = pltpu.VMEM((columns, rows), BF16)
        scratch[f"slope{t}"] = pltpu.VMEM((hidden, rows), F32)
        scratch[f"act{t}"] = pltpu.VMEM((hidden, rows), BF16)
        scratch[f"grad{t}"] = pltpu.VMEM((hidden, rows), BF16)
        scratch[f"part{t}"] = pltpu.VMEM((2, 2, columns, rows), BF16)
        scratch[f"from_core{t}"] = pltpu.VMEM((2, columns, rows), BF16)
        scratch[f"from_x{t}"] = pltpu.VMEM((columns, rows), BF16)
        scratch[f"res{t}"] = pltpu.VMEM((features, rows), BF16)
        for i, size in ((2 * t, features // stores), (2 * t + 1, width // stores)):
            shape = (hidden, size) if i == 0 else (size, hidden)
            outputs[f"out{i}"] = jax.ShapeDtypeStruct(shape, F32)
            scratch[f"sum{i}"] = pltpu.VMEM((2, 2, 2, size, hidden), BF16)
            scratch[f"first{i}"] = pltpu.VMEM((2, 2, size, hidden), BF16)
            scratch[f"next{i}"] = pltpu.VMEM((2, size, hidden), BF16)
            scratch[f"last{i}"] = pltpu.VMEM((size, hidden), BF16)
            orders.append((2, 1, 4) if i in (0, 5) else (1, 2, 4))
    for name, value in loaded.items():
        scratch[name] = pltpu.VMEM(value.shape, BF16)
    held = [name + "_hbm" for name in loaded]
    names = list(inputs) + held + list(outputs) + list(scratch)
    vmem = pl.BlockSpec(memory_space=pltpu.VMEM)
    features = sum(project.shape[1] for project in projects)
    results = pl.pallas_call(
        functools.partial(fused_kernel, names, list(loaded), orders, capacity, patches),
        out_shape=tuple(outputs.values()),
        in_specs=[vmem] * len(inputs) + [pl.BlockSpec(memory_space=pltpu.HBM)] * len(loaded),
        out_specs=tuple([vmem] * len(outputs)),
        scratch_shapes=list(scratch.values()),
        compiler_params=pltpu.CompilerParams(
            collective_id=0, has_side_effects=True, vmem_limit_bytes=60 * 1024 * 1024
        ),
        cost_estimate=pl.CostEstimate(
            flops=6 * rows * hidden * (features + 3 * width),
            bytes_accessed=16 * 1024 * 1024,
            transcendentals=6 * rows * hidden,
        ),
    )(*inputs.values(), *loaded.values())
    anywhere = pl.BlockSpec(memory_space=pltpu.HBM)
    results = pl.pallas_call(
        copy_kernel,
        out_shape=tuple(outputs.values()),
        in_specs=[anywhere] * len(outputs),
        out_specs=tuple([anywhere] * len(outputs)),
        scratch_shapes=[pltpu.VMEM(value.shape, value.dtype) for value in outputs.values()]
        + [pltpu.SemaphoreType.DMA((len(outputs),))] * 2,
        compiler_params=pltpu.CompilerParams(vmem_limit_bytes=60 * 1024 * 1024),
    )(*results)
    student_grad = results[0].reshape(student.shape[0], patches, quarter)
    return (
        student_grad,
        results[6],
        results[5].T,
        results[4],
        results[3].T,
        results[2],
        results[1],
    )


def kernel_fits(mesh):
    return mesh.shape["dp"] == 8 and mesh.shape["mp"] == 4


def solution(mesh):
    return jax.shard_map(
        fused if kernel_fits(mesh) else shards,
        mesh=mesh,
        in_specs=(
            P("dp", None, None),
            P("dp", None, "mp"),
            P("dp", None, "mp"),
            P("dp", None, "mp"),
            P(),
            P(),
            P(None, "mp"),
            P("mp", None),
            P(None, "mp"),
            P("mp", None),
            P(None, "mp"),
            P("mp", None),
        ),
        out_specs=(
            P("dp", None, "mp"),
            P("dp", "mp"),
            P("mp", "dp"),
            P("dp", "mp"),
            P("mp", "dp"),
            P("dp", "mp"),
            P("mp", "dp"),
        ),
        check_vma=False,
    )
```

```python
import functools

import jax
import jax.numpy as jnp
from jax import lax
from jax.experimental import pallas as pl
from jax.experimental.pallas import tpu as pltpu
from jax.sharding import PartitionSpec as P

MESH = pl.DeviceIdType.MESH
F32 = jnp.float32
BF16 = jnp.bfloat16


def for_sending(value):

    def short(part):
        return part.astype(jnp.bfloat16) if part.dtype == jnp.float32 else part

    return jax.tree.map(short, value)


def gelu_parts(hidden):
    normal_cdf = 0.5 * (1.0 + jax.scipy.special.erf(hidden * 0.7071067811865476))
    density = jnp.exp(-0.5 * hidden * hidden) * 0.3989422804014327
    return (hidden * normal_cdf, normal_cdf + hidden * density)


def selection(store_block, owner_ids, capacity):
    belongs = (owner_ids[:, None] == store_block[None, :]).astype(jnp.int32)
    position = jnp.cumsum(belongs, axis=1) - 1
    ranks = jnp.arange(capacity, dtype=jnp.int32)
    return belongs[:, None, :] * (position[:, None, :] == ranks[None, :, None]).astype(jnp.int32)


def fold_step(activated, project, segment):
    back_sum = lax.dot_general(
        segment, project, (((1,), (1,)), ((), ())), preferred_element_type=jnp.float32
    )
    update = lax.dot_general(
        activated, segment, (((0,), (0,)), ((), ())), preferred_element_type=jnp.float32
    )
    return (back_sum, update)


def first_term(inputs, hidden_grad, loss_scale):
    return (
        lax.dot_general(
            inputs, hidden_grad, (((0,), (0,)), ((), ())), preferred_element_type=jnp.float32
        )
        * loss_scale
    )


def adapt(inputs, targets, slot_counts, weights, loss_scale):
    positions = jnp.arange(targets[0].shape[2], dtype=jnp.int32)
    valid_mask = (
        (positions[None, None, :] < slot_counts[:, :, None]).astype(jnp.float32).reshape(-1)
    )
    student_part = jnp.zeros(inputs.shape, jnp.float32)
    results = []
    for target, weight_pair in zip(targets, weights):
        expand, project = weight_pair
        hidden = jnp.dot(inputs, expand, preferred_element_type=jnp.float32)
        activated, gelu_slope = gelu_parts(hidden)
        activated = activated.astype(jnp.bfloat16)
        adapted = lax.psum_scatter(
            jnp.dot(activated, project, preferred_element_type=jnp.float32).astype(jnp.bfloat16),
            "mp",
            scatter_dimension=1,
            tiled=True,
        ).astype(jnp.float32)
        target_flat = target.reshape(-1, target.shape[3]).astype(jnp.float32)
        residual = ((adapted - target_flat) * valid_mask[:, None]).astype(jnp.bfloat16)
        back_sum, project_grad = fold_step(
            activated, project, lax.all_gather(residual, "mp", axis=1, tiled=True)
        )
        hidden_grad = (back_sum * gelu_slope).astype(jnp.bfloat16)
        expand_grad = lax.psum_scatter(
            first_term(inputs, hidden_grad, loss_scale).astype(jnp.bfloat16),
            "dp",
            scatter_dimension=0,
            tiled=True,
        ).astype(jnp.float32)
        project_grad = lax.psum_scatter(
            (project_grad * loss_scale).astype(jnp.bfloat16), "dp", scatter_dimension=1, tiled=True
        ).astype(jnp.float32)
        student_part = student_part + lax.dot_general(
            hidden_grad, expand, (((1,), (1,)), ((), ())), preferred_element_type=jnp.float32
        )
        results.append(expand_grad)
        results.append(project_grad)
    return (student_part, results)


def shards(
    student,
    dino_target,
    siglip_target,
    clip_target,
    image_owner,
    patch_count,
    dino_expand,
    dino_project,
    siglip_expand,
    siglip_project,
    clip_expand,
    clip_project,
):
    stores = lax.axis_size("dp")
    store_index = lax.axis_index("dp")
    per_store = dino_target.shape[0]
    patches = dino_target.shape[1]
    slot_total = student.shape[0]
    capacity = slot_total // stores
    owners = image_owner[:, 0]
    store_owner = owners.reshape(stores, per_store)
    counts_store = patch_count.reshape(stores, per_store)
    loss_scale = 1.0 / jnp.sqrt(jnp.sum(patch_count).astype(jnp.float32))
    own_block = lax.dynamic_slice_in_dim(owners, store_index * per_store, per_store)
    sel_store = selection(own_block, jnp.arange(stores, dtype=jnp.int32), capacity)
    picker = sel_store.astype(jnp.bfloat16)
    teachers = (dino_target, siglip_target, clip_target)
    weights = (
        (dino_expand, dino_project),
        (siglip_expand, siglip_project),
        (clip_expand, clip_project),
    )
    outgoing = tuple(
        (
            jnp.einsum("oki,ipf->okpf", picker, teacher, preferred_element_type=jnp.float32).astype(
                jnp.bfloat16
            )
            for teacher in teachers
        )
    )
    targets = jax.tree.map(
        lambda part, own: part.astype(own.dtype),
        lax.all_to_all(for_sending(outgoing), "dp", split_axis=0, concat_axis=0, tiled=True),
        outgoing,
    )
    owner_key = jnp.reshape(store_index, (1,))
    sel_owner = jax.vmap(lambda store_block: selection(store_block, owner_key, capacity)[0])(
        store_owner
    )
    slot_counts = jnp.sum(sel_owner * counts_store[:, None, :], axis=2)
    inputs = student.reshape(-1, student.shape[2])
    student_part, results = adapt(inputs, targets, slot_counts, weights, loss_scale)
    student_grad = lax.psum_scatter(
        student_part.reshape(slot_total, patches, -1).astype(jnp.bfloat16),
        "mp",
        scatter_dimension=2,
        tiled=True,
    )
    return (student_grad, results[0], results[1], results[2], results[3], results[4], results[5])


def nn(a, b):
    return lax.dot_general(a, b, (((1,), (0,)), ((), ())), preferred_element_type=F32)


def nt(a, b):
    return lax.dot_general(a, b, (((1,), (1,)), ((), ())), preferred_element_type=F32)


def tn(a, b):
    return lax.dot_general(a, b, (((0,), (0,)), ((), ())), preferred_element_type=F32)


def rows_at(index, size):
    return pl.ds(pl.multiple_of(index * size, 16), size)


def fused_kernel(names, names_loaded, orders, capacity, patches, *refs):
    r = dict(zip(names, refs))
    dp, mp = lax.axis_index("dp"), lax.axis_index("mp")
    x, core = mp // 2, mp % 2
    sibling = mp + 1 - 2 * core
    across = mp + 2 - 4 * x
    n_dp, n_mp = 8, 4
    sent = []
    numbers = iter(range(r["ssem"].shape[0]))

    def send(source, landing, device):
        number = next(numbers)
        copy = pltpu.make_async_remote_copy(
            src_ref=source,
            dst_ref=landing,
            send_sem=r["ssem"].at[number],
            recv_sem=r["rsem"].at[number],
            device_id=device,
            device_id_type=MESH,
        )
        copy.start()
        sent.append(copy)
        return copy

    loads = {}
    for number, name in enumerate(names_loaded):
        loads[name] = pltpu.make_async_copy(r[name + "_hbm"], r[name], r["lsem"].at[number])
        loads[name].start()

    dp_peers = [lax.rem(dp + k, n_dp) for k in range(1, n_dp)]
    barrier = pltpu.get_barrier_semaphore()
    for peer in dp_peers:
        pl.semaphore_signal(barrier, inc=1, device_id=(peer, mp), device_id_type=MESH)
    for peer in (sibling, across):
        pl.semaphore_signal(barrier, inc=1, device_id=(dp, peer), device_id_type=MESH)
    pl.semaphore_wait(barrier, n_dp + 1)

    xs, xr, xt = r["xs"], r["xr"], r["xt"]
    quarter = xt.shape[0] // n_mp
    slot_rows, row_total = xr.shape[0] * xr.shape[1], xt.shape[1]
    arrivals = [send(xs.at[peer], xr.at[dp], (peer, mp)) for peer in dp_peers]
    xr[dp] = xs[dp]

    owners, counts = r["owners"][...], r["counts"][...]
    images = owners.shape[1]
    per_store = row_total // patches
    first_image = dp * per_store
    image = lax.broadcasted_iota(jnp.int32, (images, row_total), 0) - first_image
    column = lax.broadcasted_iota(jnp.int32, (images, row_total), 1)
    at_column = column // patches
    same = (image == at_column).astype(F32).astype(BF16)
    before = ((image >= 0) & (image < at_column)).astype(F32).astype(BF16)
    padded = jnp.broadcast_to(owners, (8, images))
    owner_of = nn(padded.astype(F32).astype(BF16), same)
    count_of = nn(jnp.broadcast_to(counts, (8, images)).astype(F32).astype(BF16), same)
    named = lax.broadcasted_iota(jnp.int32, (n_dp, images), 0) == padded
    ranks = nn(named.astype(F32).astype(BF16), before)
    ours = lax.broadcasted_iota(jnp.int32, (n_dp, row_total), 0) == owner_of.astype(jnp.int32)
    rank = jnp.sum(jnp.where(ours, ranks, 0.0), axis=0, keepdims=True)
    patch = column[:1] - at_column[:1] * patches
    slot = owner_of[:1].astype(jnp.int32) * capacity + rank.astype(jnp.int32)
    r["valid"][...] = (patch < count_of[:1].astype(jnp.int32)).astype(F32)
    total = jnp.sum(counts.astype(F32), axis=1, keepdims=True)
    r["scale"][...] = jnp.broadcast_to(1.0 / jnp.sqrt(total), r["scale"].shape)
    place = slot * patches + patch
    picked = lax.broadcasted_iota(jnp.int32, (slot_rows, row_total), 0) == place
    r["sel"][...] = picked.astype(F32).astype(BF16)

    def turn(t):
        for kind in ("expand", "project", "target"):
            loads[f"{kind}{t}"].wait()
            r[f"{kind}_t{t}"][...] = r[f"{kind}{t}"][...].T

    turn(0)
    for copy in arrivals:
        copy.wait_recv()
    mine = rows_at(mp, quarter)
    theirs = rows_at(across, quarter)
    xt[mine, :] = tn(xr[...].reshape(slot_rows, quarter), r["sel"][...]).astype(BF16)
    to_sibling = send(xt.at[mine, :], xt.at[mine, :], (dp, sibling))
    to_across = send(xt.at[mine, :], xt.at[mine, :], (dp, across))
    turn(1)
    to_across.wait_recv()
    forward = send(xt.at[theirs, :], xt.at[theirs, :], (dp, sibling))
    to_sibling.wait_recv()
    forward.wait_recv()

    teachers = range(3)
    core_copy, x_copy, gather = {}, {}, {}

    def first_half(t):
        project_t = r[f"project_t{t}"]
        hidden = nn(r[f"expand_t{t}"][...], xt[...])
        cdf = 0.5 * (1.0 + lax.erf(hidden * 0.7071067811865476))
        density = jnp.exp(-0.5 * hidden * hidden) * 0.3989422804014327
        r[f"slope{t}"][...] = cdf + hidden * density
        r[f"act{t}"][...] = (hidden * cdf).astype(BF16)
        part = r[f"part{t}"]
        width = part.shape[2]

        def block(j, carry):
            part[j % 2, j // 2] = nn(
                project_t[rows_at(j, width), :], r[f"act{t}"][...]
            ).astype(BF16)
            return carry

        lax.fori_loop(0, n_mp, block, 0)
        core_copy[t] = send(part.at[1 - core], r[f"from_core{t}"], (dp, sibling))

    def to_x(t):
        part, landed = r[f"part{t}"], r[f"from_core{t}"]
        core_copy[t].wait_recv()
        part[core, 1 - x] = (
            part[core, 1 - x].astype(F32) + landed[1 - x].astype(F32)
        ).astype(BF16)
        x_copy[t] = send(part.at[core, 1 - x], r[f"from_x{t}"], (dp, across))

    def residual(t):
        part, landed, res = r[f"part{t}"], r[f"from_core{t}"], r[f"res{t}"]
        width = part.shape[2]
        own = part[core, x].astype(F32) + landed[x].astype(F32)
        x_copy[t].wait_recv()
        adapted = own + r[f"from_x{t}"][...].astype(F32)
        here = rows_at(mp, width)
        res[here, :] = ((adapted - r[f"target_t{t}"][...].astype(F32)) * r["valid"][...]).astype(BF16)
        near = send(res.at[here, :], res.at[here, :], (dp, sibling))
        far = send(res.at[here, :], res.at[here, :], (dp, across))
        gather[t] = (near, far)

    def pass_on(t):
        res = r[f"res{t}"]
        there = rows_at(across, r[f"part{t}"].shape[2])
        near, far = gather[t]
        far.wait_recv()
        gather[t] = (near, send(res.at[there, :], res.at[there, :], (dp, sibling)))

    def bit_of(index, bit):
        return (index // bit) % 2

    def partner(bit):
        return dp + bit - 2 * bit * bit_of(dp, bit)

    stage = {}

    def start_reduce(i):
        total, order = r[f"sum{i}"], orders[i]
        stage[i] = send(
            total.at[1 - bit_of(dp, order[0])], r[f"first{i}"], (partner(order[0]), mp)
        )

    def second(i):
        total, landed, order = r[f"sum{i}"], r[f"first{i}"], orders[i]
        own = bit_of(dp, order[0])
        stage[i].wait_recv()

        def block(k, carry):
            a, b = k // 2, k % 2
            total[own, a, b] = total[own, a, b] + landed[a, b]
            return carry

        lax.fori_loop(0, 4, block, 0)
        stage[i] = send(
            total.at[own, 1 - bit_of(dp, order[1])], r[f"next{i}"], (partner(order[1]), mp)
        )

    def third(i):
        total, landed, order = r[f"sum{i}"], r[f"next{i}"], orders[i]
        own, mid = bit_of(dp, order[0]), bit_of(dp, order[1])
        stage[i].wait_recv()

        def block(k, carry):
            total[own, mid, k] = total[own, mid, k] + landed[k]
            return carry

        lax.fori_loop(0, 2, block, 0)
        stage[i] = send(
            total.at[own, mid, 1 - bit_of(dp, order[2])], r[f"last{i}"], (partner(order[2]), mp)
        )

    def finish(i):
        total, order = r[f"sum{i}"], orders[i]
        own = [bit_of(dp, bit) for bit in order]
        stage[i].wait_recv()
        summed = (
            total[own[0], own[1], own[2]].astype(F32) + r[f"last{i}"][...].astype(F32)
        ) * r["scale"][...]
        r[f"out{i}"][...] = summed.T if i == 0 else summed

    def weight_grad(i, left, right):
        total, order = r[f"sum{i}"], orders[i]
        size = total.shape[3]

        def block(k, carry):
            both = nt(left[rows_at(k, 2 * size), :], right[...]).astype(BF16)
            for low in (0, 1):
                at = [bit_of(2 * k + low, bit) for bit in order]
                total[at[0], at[1], at[2]] = both[low * size : (low + 1) * size]
            return carry

        lax.fori_loop(0, n_dp // 2, block, 0)

    def project_grad(t):
        near, forwarded = gather[t]
        near.wait_recv()
        forwarded.wait_recv()
        weight_grad(2 * t, r[f"res{t}"], r[f"act{t}"])
        start_reduce(2 * t)

    def hidden_grad(t):
        back = nn(r[f"project{t}"][...], r[f"res{t}"][...])
        r[f"grad{t}"][...] = (back * r[f"slope{t}"][...]).astype(BF16)

    def expand_grad(t):
        weight_grad(2 * t + 1, xt, r[f"grad{t}"])

    first_half(0)
    to_x(0)
    first_half(1)
    residual(0)
    turn(2)
    first_half(2)
    pass_on(0)
    to_x(1)
    project_grad(0)
    hidden_grad(0)
    expand_grad(0)
    start_reduce(1)
    residual(1)
    second(0)
    pass_on(1)
    to_x(2)
    project_grad(1)
    hidden_grad(1)
    expand_grad(1)
    second(1)
    third(0)
    residual(2)
    second(2)
    start_reduce(3)
    pass_on(2)
    project_grad(2)
    hidden_grad(2)

    sp = r["sp"]

    def block(j, carry):
        sp[j % 2, j // 2] = sum(
            nn(r[f"expand{t}"][rows_at(j, quarter), :], r[f"grad{t}"][...]) for t in teachers
        ).astype(BF16)
        return carry

    lax.fori_loop(0, n_mp, block, 0)
    core_copy["s"] = send(sp.at[1 - core], r["sp_core"], (dp, sibling))
    expand_grad(2)
    start_reduce(5)
    core_copy["s"].wait_recv()
    sp[core, 1 - x] = (
        sp[core, 1 - x].astype(F32) + r["sp_core"][1 - x].astype(F32)
    ).astype(BF16)
    x_copy["s"] = send(sp.at[core, 1 - x], r["sp_x"], (dp, across))
    third(1)
    second(3)
    third(2)
    finish(0)
    own = sp[core, x].astype(F32) + r["sp_core"][x].astype(F32)
    x_copy["s"].wait_recv()
    summed = (own + r["sp_x"][...].astype(F32)).astype(BF16)
    placed = nt(r["sel"][...], summed).astype(BF16)
    r["home"][...] = placed.reshape(r["home"].shape)
    returns = [
        send(r["home"].at[peer], r["student_out"].at[dp], (peer, mp)) for peer in dp_peers
    ]
    r["student_out"][dp] = r["home"][dp]
    finish(1)
    third(3)
    second(5)
    finish(2)
    second(4)
    finish(3)
    third(5)
    third(4)
    finish(5)
    finish(4)
    for copy in returns:
        copy.wait_recv()
    for copy in sent:
        copy.wait_send()


def copy_kernel(*refs):
    count = len(refs) // 3
    sources, results, held = refs[:count], refs[count : 2 * count], refs[2 * count : 3 * count]
    entry, leave = refs[3 * count :]
    arrive = [pltpu.make_async_copy(sources[i], held[i], entry.at[i]) for i in range(count)]
    depart = [pltpu.make_async_copy(held[i], results[i], leave.at[i]) for i in range(count)]
    for copy in arrive:
        copy.start()
    for i in range(count):
        arrive[i].wait()
        depart[i].start()
    for copy in depart:
        copy.wait()


def fused(
    student,
    dino_target,
    siglip_target,
    clip_target,
    image_owner,
    patch_count,
    dino_expand,
    dino_project,
    siglip_expand,
    siglip_project,
    clip_expand,
    clip_project,
):
    stores, groups = lax.axis_size("dp"), lax.axis_size("mp")
    mp = lax.axis_index("mp")
    per_store, patches = dino_target.shape[0], dino_target.shape[1]
    capacity = student.shape[0] // stores
    width = student.shape[2]
    quarter = width // groups
    rows = per_store * patches
    hidden = dino_expand.shape[1]
    xs = lax.dynamic_slice_in_dim(
        student.reshape(stores, capacity * patches, width), mp * quarter, quarter, axis=2
    )
    expands = (clip_expand, siglip_expand, dino_expand)
    projects = (clip_project, siglip_project, dino_project)
    targets = (clip_target, siglip_target, dino_target)

    inputs = {
        "xs": xs,
        "owners": image_owner.reshape(1, -1),
        "counts": patch_count.reshape(1, -1),
    }
    loaded = {}
    outputs = {"student_out": jax.ShapeDtypeStruct(xs.shape, BF16)}
    scratch = {
        "ssem": pltpu.SemaphoreType.DMA((52,)),
        "rsem": pltpu.SemaphoreType.DMA((52,)),
        "lsem": pltpu.SemaphoreType.DMA((9,)),
        "valid": pltpu.VMEM((1, rows), F32),
        "scale": pltpu.VMEM((1, hidden), F32),
        "xr": pltpu.VMEM(xs.shape, BF16),
        "home": pltpu.VMEM(xs.shape, BF16),
        "xt": pltpu.VMEM((width, rows), BF16),
        "sel": pltpu.VMEM((stores * capacity * patches, rows), BF16),
        "sp": pltpu.VMEM((2, 2, quarter, rows), BF16),
        "sp_core": pltpu.VMEM((2, quarter, rows), BF16),
        "sp_x": pltpu.VMEM((quarter, rows), BF16),
    }
    orders = []
    for t, (target, expand, project) in enumerate(zip(targets, expands, projects)):
        columns = target.shape[2]
        features = project.shape[1]
        loaded[f"expand{t}"] = expand
        loaded[f"project{t}"] = project
        loaded[f"target{t}"] = target.reshape(rows, columns)
        scratch[f"expand_t{t}"] = pltpu.VMEM(expand.shape[::-1], BF16)
        scratch[f"project_t{t}"] = pltpu.VMEM(project.shape[::-1], BF16)
        scratch[f"target_t{t}"] = pltpu.VMEM((columns, rows), BF16)
        scratch[f"slope{t}"] = pltpu.VMEM((hidden, rows), F32)
        scratch[f"act{t}"] = pltpu.VMEM((hidden, rows), BF16)
        scratch[f"grad{t}"] = pltpu.VMEM((hidden, rows), BF16)
        scratch[f"part{t}"] = pltpu.VMEM((2, 2, columns, rows), BF16)
        scratch[f"from_core{t}"] = pltpu.VMEM((2, columns, rows), BF16)
        scratch[f"from_x{t}"] = pltpu.VMEM((columns, rows), BF16)
        scratch[f"res{t}"] = pltpu.VMEM((features, rows), BF16)
        for i, size in ((2 * t, features // stores), (2 * t + 1, width // stores)):
            shape = (hidden, size) if i == 0 else (size, hidden)
            outputs[f"out{i}"] = jax.ShapeDtypeStruct(shape, F32)
            scratch[f"sum{i}"] = pltpu.VMEM((2, 2, 2, size, hidden), BF16)
            scratch[f"first{i}"] = pltpu.VMEM((2, 2, size, hidden), BF16)
            scratch[f"next{i}"] = pltpu.VMEM((2, size, hidden), BF16)
            scratch[f"last{i}"] = pltpu.VMEM((size, hidden), BF16)
            orders.append((2, 1, 4) if i in (0, 5) else (1, 2, 4))
    for name, value in loaded.items():
        scratch[name] = pltpu.VMEM(value.shape, BF16)
    held = [name + "_hbm" for name in loaded]
    names = list(inputs) + held + list(outputs) + list(scratch)
    vmem = pl.BlockSpec(memory_space=pltpu.VMEM)
    features = sum(project.shape[1] for project in projects)
    results = pl.pallas_call(
        functools.partial(fused_kernel, names, list(loaded), orders, capacity, patches),
        out_shape=tuple(outputs.values()),
        in_specs=[vmem] * len(inputs) + [pl.BlockSpec(memory_space=pltpu.HBM)] * len(loaded),
        out_specs=tuple([vmem] * len(outputs)),
        scratch_shapes=list(scratch.values()),
        compiler_params=pltpu.CompilerParams(
            collective_id=0, has_side_effects=True, vmem_limit_bytes=60 * 1024 * 1024
        ),
        cost_estimate=pl.CostEstimate(
            flops=6 * rows * hidden * (features + 3 * width),
            bytes_accessed=16 * 1024 * 1024,
            transcendentals=6 * rows * hidden,
        ),
    )(*inputs.values(), *loaded.values())
    anywhere = pl.BlockSpec(memory_space=pltpu.HBM)
    results = pl.pallas_call(
        copy_kernel,
        out_shape=tuple(outputs.values()),
        in_specs=[anywhere] * len(outputs),
        out_specs=tuple([anywhere] * len(outputs)),
        scratch_shapes=[pltpu.VMEM(value.shape, value.dtype) for value in outputs.values()]
        + [pltpu.SemaphoreType.DMA((len(outputs),))] * 2,
        compiler_params=pltpu.CompilerParams(vmem_limit_bytes=60 * 1024 * 1024),
    )(*results)
    student_grad = results[0].reshape(student.shape[0], patches, quarter)
    return (
        student_grad,
        results[6],
        results[5].T,
        results[4],
        results[3].T,
        results[2],
        results[1],
    )


def kernel_fits(mesh):
    return mesh.shape["dp"] == 8 and mesh.shape["mp"] == 4


def solution(mesh):
    return jax.shard_map(
        fused if kernel_fits(mesh) else shards,
        mesh=mesh,
        in_specs=(
            P("dp", None, None),
            P("dp", None, "mp"),
            P("dp", None, "mp"),
            P("dp", None, "mp"),
            P(),
            P(),
            P(None, "mp"),
            P("mp", None),
            P(None, "mp"),
            P("mp", None),
            P(None, "mp"),
            P("mp", None),
        ),
        out_specs=(
            P("dp", None, "mp"),
            P("dp", "mp"),
            P("mp", "dp"),
            P("dp", "mp"),
            P("mp", "dp"),
            P("dp", "mp"),
            P("mp", "dp"),
        ),
        check_vma=False,
    )
```
